512 devices in a mesh: ctx: 64 (over z, y_lo, core), tp: 8 (over y_hi, x).
Axes of the slice: x: 4, y: 4 (y_hi: 2, y_lo: 2; y = y_hi * 2 + y_lo), z: 16, core: 2. Of those that a mesh axis runs over, the one named last changes fastest.
Arguments:
- queries: bfloat16 [8192, 32, 128], P('ctx', 'tp'), may hold values from -20 to 20
- prompt_kv: bfloat16 [16384, 2, 8, 128], P('ctx', None, 'tp'), may hold values from -20 to 20
- response_kv: bfloat16 [8192, 2, 8, 128], P('ctx', None, 'tp'), may hold values from -6 to 6
- logits: bfloat16 [8192, 76800], P('ctx', 'tp'), may hold values from -330 to 330
- token_ids: int32 [8192], P('ctx'), may hold values from 0 to 76799
- lengths: int32 [16], replicated, may hold values from 1 to 2048, as said below
- rewards: float32 [16], replicated, may hold values from -4 to 4
Outputs:
- context: bfloat16 [8192, 32, 128], P('ctx', 'tp')
- token_logprob: float32 [8192], P('ctx')
- response_objective: float32 [16], replicated
The draws below stay inside these ranges and needn't reach their ends.
Inputs may be any that keep to these rules, and one draw needn't show every extreme that they name: The lengths sum to 8128; the last response has exactly 2048 rows.
All inputs are finite; a program needn't handle non-finite values.
Results may differ from the reference program's by a relative error of at most 0.01.
Values may be sent and summed in bfloat16 or wider, within the bound.
No kernel may reach another device: no remote copies, remote signals or barrier semaphores. Data moves between devices by JAX's collectives and lax.ppermute only.
A program may use at most 64 MiB of HBM per device.

```python
import math
import jax
import jax.numpy as jnp
from jax import lax

QH = 32
KVH = 8
HD = 128
VOCAB = 76800
RESPONSES = 16
ROWS = 8192
PROMPT = 16384
RESP_MAX = 2048
PACKED = 8128


def draw_queries(key, part):
    key = jax.random.fold_in(key, 11)
    values = jax.random.truncated_normal(key, -5.0, 5.0, (ROWS, QH, HD), jnp.float32)
    return values.astype(jnp.bfloat16)


def draw_prompt_kv(key, part):
    key = jax.random.fold_in(key, 13)
    shape = (PROMPT, 2, KVH, HD)
    values = jax.random.truncated_normal(key, -5.0, 5.0, shape, jnp.float32)
    return values.astype(jnp.bfloat16)


def draw_logits(key, part):
    key = jax.random.fold_in(key, 23)
    base_key, column_key, row_key = jax.random.split(key, 3)
    column_scale = jnp.exp(jax.random.uniform(column_key, (VOCAB,), jnp.float32, -1.15, 1.15))
    row_scale = jnp.exp(jax.random.uniform(row_key, (ROWS,), jnp.float32, -0.35, 0.35))
    values = jax.random.truncated_normal(base_key, -5.0, 5.0, (ROWS, VOCAB), jnp.float32) * 3.0 * row_scale[:, None] * column_scale[None, :]
    return values.astype(jnp.bfloat16)


def draw_lengths(key, part):
    key = jax.random.fold_in(key, 31)
    others = RESPONSES - 1
    surplus = PACKED - RESP_MAX - others
    headroom = RESP_MAX - 1
    drawn = jax.random.randint(key, (others,), 1, 17, dtype=jnp.int32)
    weights = drawn * drawn
    total_weight = jnp.sum(weights)
    additions = jnp.minimum(headroom, surplus * weights // total_weight).astype(jnp.int32)
    remaining = surplus - jnp.sum(additions)
    for position in range(others):
        granted = jnp.minimum(headroom - additions[position], remaining)
        additions = additions.at[position].add(granted)
        remaining = remaining - granted
    final_length = jnp.full((1,), RESP_MAX, jnp.int32)
    return jnp.concatenate([1 + additions, final_length]).astype(jnp.int32)


def with_ends(result, stream_key, least, largest):
    longest = result.shape.index(max(result.shape))
    spots = []
    for shift in (0, 1):
        where = [jax.random.randint(jax.random.fold_in(stream_key, axis), (), 0, length) for axis, length in enumerate(result.shape)]
        where[longest] = (where[longest] + shift) % result.shape[longest]
        spots.append(tuple(where))
    return result.at[spots[0]].set(least).at[spots[1]].set(largest)


def level_of(own_key, shape, pieces, least, top_value):
    factor_of, own = 1.0, jax.random.fold_in(own_key, 6)
    for axis_at, parts in pieces:
        heights = jnp.exp(jax.random.uniform(jax.random.fold_in(own, axis_at), (parts,), jnp.float32, least / len(pieces), top_value / len(pieces)))
        factor_of = factor_of * jnp.repeat(heights, shape[axis_at] // parts).reshape([-1 if axis == axis_at else 1 for axis in range(len(shape))])
    return factor_of


def gaussian(rng, dims, scale, bound, cuts=(), held_as=jnp.bfloat16):
    loudness = level_of(rng, dims, cuts, -0.22, 0.18) if cuts else 1.0
    values = jax.random.normal(rng, dims, jnp.float32) * scale * loudness
    return jnp.minimum(jnp.maximum(values, -bound), bound).astype(held_as)


def setup_inputs(seed: int = 0) -> dict:
    splits = jax.random.split(jax.random.key(seed), 8)
    return {
        "queries": draw_queries(jax.random.fold_in(splits[7], 71), 0),
        "prompt_kv": draw_prompt_kv(jax.random.fold_in(splits[7], 71), 0),
        "response_kv": gaussian(splits[2], (ROWS, 2, KVH, HD), 1.0, 6.0, ((0, 64), (2, 8))),
        "logits": draw_logits(jax.random.fold_in(splits[7], 71), 0),
        "token_ids": with_ends(jax.random.randint(splits[4], (ROWS,), 0, VOCAB), jax.random.fold_in(splits[4], 1), 0, VOCAB - 1).astype(jnp.int32),
        "lengths": draw_lengths(jax.random.fold_in(splits[7], 71), 0),
        "rewards": gaussian(splits[6], (RESPONSES,), 1.0, 4.0, (), jnp.float32),
    }


def segment_of(row_index, lengths):
    ends_at = jnp.cumsum(lengths).astype(jnp.int32)
    return lax.optimization_barrier(jnp.sum((row_index[:, None] >= ends_at[None, :]).astype(jnp.int32), axis=1))

def reference(queries, prompt_kv, response_kv, logits, token_ids, lengths, rewards):
    all_rows = jnp.arange(ROWS, dtype=jnp.int32)
    segments = segment_of(all_rows, lengths)
    score_scale = 1.0 / math.sqrt(HD)
    group_size = QH // KVH
    block_rows = math.gcd(ROWS, 512)
    block_count = ROWS // block_rows

    def attend(flat_index):
        block_index = flat_index // KVH
        head_index = flat_index % KVH
        row_start = (block_index * block_rows).astype(jnp.int32)
        head_start = (head_index * group_size).astype(jnp.int32)
        query_part = lax.dynamic_slice(queries, (row_start, head_start, jnp.int32(0)), (block_rows, group_size, HD)).astype(jnp.float32)
        prompt_keys = lax.dynamic_index_in_dim(prompt_kv[:, 0], head_index, axis=1, keepdims=False).astype(jnp.float32)
        prompt_values = lax.dynamic_index_in_dim(prompt_kv[:, 1], head_index, axis=1, keepdims=False).astype(jnp.float32)
        own_keys = lax.dynamic_index_in_dim(response_kv[:, 0], head_index, axis=1, keepdims=False).astype(jnp.float32)
        own_values = lax.dynamic_index_in_dim(response_kv[:, 1], head_index, axis=1, keepdims=False).astype(jnp.float32)
        query_rows = row_start + jnp.arange(block_rows, dtype=jnp.int32)
        query_seg = lax.dynamic_slice_in_dim(segments, row_start, block_rows)
        visible = (segments[None, :] == query_seg[:, None]) & (query_seg[:, None] < RESPONSES) & (all_rows[None, :] <= query_rows[:, None]) | (all_rows[None, :] == query_rows[:, None])
        prompt_scores = jnp.einsum('bhd,pd->bhp', query_part, prompt_keys) * score_scale
        own_scores = jnp.einsum('bhd,jd->bhj', query_part, own_keys) * score_scale
        own_scores = jnp.where(visible[:, None, :], own_scores, -1e+30)
        highest = jnp.maximum(prompt_scores.max(-1), own_scores.max(-1))
        prompt_weights = jnp.exp(prompt_scores - highest[..., None])
        own_weights = jnp.where(visible[:, None, :], jnp.exp(own_scores - highest[..., None]), 0.0)
        denominator = prompt_weights.sum(-1) + own_weights.sum(-1)
        prompt_round = lax.optimization_barrier(prompt_weights.astype(jnp.bfloat16)).astype(jnp.float32)
        own_round = lax.optimization_barrier(own_weights.astype(jnp.bfloat16)).astype(jnp.float32)
        summed = jnp.einsum('bhp,pd->bhd', prompt_round, prompt_values) + jnp.einsum('bhj,jd->bhd', own_round, own_values)
        return (summed / denominator[..., None]).astype(jnp.bfloat16)
    outputs = lax.map(attend, jnp.arange(block_count * KVH, dtype=jnp.int32))
    context = outputs.reshape(block_count, KVH, block_rows, group_size, HD).transpose(0, 2, 1, 3, 4).reshape(ROWS, QH, HD)

    def vocab_block(block_index):
        row_start = (block_index * block_rows).astype(jnp.int32)
        section = lax.dynamic_slice_in_dim(logits, row_start, block_rows).astype(jnp.float32)
        chosen_ids = lax.dynamic_slice_in_dim(token_ids, row_start, block_rows)
        vocab_peak = section.max(1)
        spread = lax.optimization_barrier(jnp.sum(jnp.exp(section - vocab_peak[:, None]), axis=1))
        picked = jnp.take_along_axis(section, chosen_ids[:, None], axis=1)[:, 0]
        return picked - vocab_peak - jnp.log(spread)
    logprob = lax.map(vocab_block, jnp.arange(block_count, dtype=jnp.int32)).reshape(ROWS)
    is_valid = segments < RESPONSES
    token_logprob = jnp.where(is_valid, logprob, 0.0)
    members = segments[:, None] == jnp.arange(RESPONSES, dtype=jnp.int32)[None, :]
    response_sum = lax.optimization_barrier(jnp.sum(jnp.where(members, token_logprob[:, None], 0.0), axis=0))
    length_float = lengths.astype(jnp.float32)
    adjusted = rewards - 0.5 * length_float / RESP_MAX
    advantage = adjusted - jnp.mean(adjusted)
    response_objective = -advantage * response_sum / length_float
    return (context, token_logprob, response_objective)
```

```python
import functools
import math

import jax
import jax.numpy as jnp
from jax import lax
from jax.experimental import pallas as pl
from jax.experimental.pallas import tpu as pltpu
from jax.sharding import Mesh, PartitionSpec as P

HD = 128
HEADS = 4
ROWS_DEV = 128
PLANE = 4
TILE = 256
SCALE = 1.0 / math.sqrt(HD)
LOG2E = 1.4426950408889634
CTX = ("z", "yl", "core")
PLANE_AXES = ("yl", "core")
MIB = 1 << 20


def logit_kernel(token_ref, base_ref, logits_ref, out_ref, stat_ref):
    step = pl.program_id(0)
    rows = logits_ref.shape[0]
    width = logits_ref.shape[1]
    here = pl.ds(pl.multiple_of(step * rows, rows), rows)
    wide = logits_ref[...].astype(jnp.float32)
    peak = jnp.max(wide, axis=1, keepdims=True)
    total = jnp.sum(jnp.exp(wide - peak), axis=1, keepdims=True)
    target = token_ref[...] - base_ref[0]
    columns = lax.broadcasted_iota(jnp.int32, (rows, width), 1)
    picked = jnp.sum(jnp.where(columns == target, wide, 0.0), axis=1, keepdims=True)
    lane = lax.broadcasted_iota(jnp.int32, (rows, 128), 1)
    stat_ref[here, :] = jnp.where(
        lane == 0, peak, jnp.where(lane == 1, total, picked)
    )

    @pl.when(step == pl.num_programs(0) - 1)
    def _():
        out_ref[...] = stat_ref[...].T[:8]


def logit_stats(logits, token_ids, vocab_base):
    rows, width = logits.shape
    block = 32
    return pl.pallas_call(
        logit_kernel,
        grid=(rows // block,),
        in_specs=[
            pl.BlockSpec((block, 1), lambda i: (i, 0)),
            pl.BlockSpec(memory_space=pltpu.SMEM),
            pl.BlockSpec((block, width), lambda i: (i, 0)),
        ],
        out_specs=pl.BlockSpec((8, 128), lambda i: (0, 0)),
        out_shape=jax.ShapeDtypeStruct((8, 128), jnp.float32),
        scratch_shapes=[pltpu.VMEM((rows, 128), jnp.float32)],
        compiler_params=pltpu.CompilerParams(vmem_limit_bytes=32 * MIB),
        cost_estimate=pl.CostEstimate(
            flops=8 * rows * width, bytes_accessed=2 * rows * width, transcendentals=rows * width
        ),
        name="logit_stats",
    )(token_ids.reshape(rows, 1), vocab_base, logits)


def nt(a, b):
    return lax.dot_general(a, b, (((1,), (1,)), ((), ())), preferred_element_type=jnp.float32)


def attend_kernel(lengths_ref, place_ref, q_ref, prompt_ref, own_ref, out_ref, pv_ref, ov_ref):
    prompt_rows = prompt_ref.shape[0]
    own_rows = own_ref.shape[0]
    pv_ref[:, :HD] = prompt_ref[:, HD:]
    pv_ref[:, HD:] = jnp.ones((prompt_rows, HD), jnp.bfloat16)
    ov_ref[:, :HD] = own_ref[:, HD:]
    ov_ref[:, HD:] = jnp.ones((own_rows, HD), jnp.bfloat16)
    first_row = place_ref[0]
    first_key = place_ref[1]
    lane = lax.broadcasted_iota(jnp.int32, (TILE, HD), 1)
    key_block = lax.broadcasted_iota(jnp.int32, (TILE, own_rows), 1)
    keys = first_key + (key_block // ROWS_DEV) * (PLANE * ROWS_DEV) + key_block % ROWS_DEV
    per = TILE // ROWS_DEV

    def row_tile(t, carry):
        rows = first_row + t * TILE + lax.broadcasted_iota(jnp.int32, (TILE, 1), 0)
        start = jnp.zeros((TILE, 1), jnp.int32)
        edge = jnp.int32(0)
        for r in range(lengths_ref.shape[0]):
            edge = edge + lengths_ref[r]
            start = jnp.where(rows >= edge, edge, start)
        start = jnp.where(rows >= edge, rows, start)
        allowed = (keys >= start) & (keys <= rows)
        packed = jnp.zeros((TILE, HD), jnp.float32)
        devs = pl.ds(t * per, per)
        for h in range(HEADS):
            lanes = slice(h * HD, (h + 1) * HD)
            q = q_ref[devs, :, lanes].reshape(TILE, HD)
            s1 = nt(q, prompt_ref[:, :HD])
            s2 = jnp.where(allowed, nt(q, own_ref[:, :HD]), -1e30)
            m = jnp.maximum(
                jnp.max(s1, axis=1, keepdims=True), jnp.max(s2, axis=1, keepdims=True)
            )
            p1 = jnp.exp2((s1 - m) * (SCALE * LOG2E)).astype(jnp.bfloat16)
            p2 = jnp.exp2((s2 - m) * (SCALE * LOG2E)).astype(jnp.bfloat16)
            acc = jnp.dot(p1, pv_ref[...], preferred_element_type=jnp.float32)
            acc = acc + jnp.dot(p2, ov_ref[...], preferred_element_type=jnp.float32)
            denominator = acc[:, HD:]
            out_ref[devs, :, lanes] = (
                (acc[:, :HD] / denominator).astype(jnp.bfloat16).reshape(per, ROWS_DEV, HD)
            )
            lse = m * SCALE + jnp.log(denominator)
            high = lse.astype(jnp.bfloat16).astype(jnp.float32)
            middle = (lse - high).astype(jnp.bfloat16).astype(jnp.float32)
            low = lse - high - middle
            packed = jnp.where(lane == 3 * h, high, packed)
            packed = jnp.where(lane == 3 * h + 1, middle, packed)
            packed = jnp.where(lane == 3 * h + 2, low, packed)
        out_ref[devs, :, HEADS * HD :] = packed.astype(jnp.bfloat16).reshape(per, ROWS_DEV, HD)
        return carry

    lax.fori_loop(0, PLANE * ROWS_DEV // TILE, row_tile, 0)


def attend(lengths, place, q, prompt, own):
    vmem = pl.BlockSpec(memory_space=pltpu.VMEM)
    smem = pl.BlockSpec(memory_space=pltpu.SMEM)
    keys = prompt.shape[0] + own.shape[0]
    pairs = PLANE * ROWS_DEV * HEADS * keys
    return pl.pallas_call(
        attend_kernel,
        in_specs=[smem, smem, vmem, vmem, vmem],
        out_specs=vmem,
        out_shape=jax.ShapeDtypeStruct((PLANE, ROWS_DEV, HEADS * HD + HD), jnp.bfloat16),
        scratch_shapes=[
            pltpu.VMEM((prompt.shape[0], 2 * HD), jnp.bfloat16),
            pltpu.VMEM((own.shape[0], 2 * HD), jnp.bfloat16),
        ],
        compiler_params=pltpu.CompilerParams(vmem_limit_bytes=48 * MIB),
        cost_estimate=pl.CostEstimate(
            flops=4 * HD * pairs, bytes_accessed=512 * keys + 2 * MIB, transcendentals=pairs
        ),
        name="attend",
    )(lengths, place, q, prompt, own)


def combine_kernel(parts_ref, out_ref):
    for h in range(HEADS):
        lanes = slice(h * HD, (h + 1) * HD)
        lse = []
        for j in range(PLANE):
            base = HEADS * HD + 3 * h
            bits = parts_ref[j, :, HEADS * HD :].astype(jnp.float32)
            lse.append(
                bits[:, 3 * h : 3 * h + 1] + bits[:, 3 * h + 1 : 3 * h + 2] + bits[:, 3 * h + 2 : 3 * h + 3]
            )
        top = jnp.maximum(jnp.maximum(lse[0], lse[1]), jnp.maximum(lse[2], lse[3]))
        weights = [jnp.exp(x - top) for x in lse]
        share = 1.0 / (weights[0] + weights[1] + weights[2] + weights[3])
        total = sum(
            (weights[j] * share) * parts_ref[j, :, lanes].astype(jnp.float32) for j in range(PLANE)
        )
        out_ref[:, lanes] = total.astype(jnp.bfloat16)


def combine(parts):
    vmem = pl.BlockSpec(memory_space=pltpu.VMEM)
    return pl.pallas_call(
        combine_kernel,
        in_specs=[vmem],
        out_specs=vmem,
        out_shape=jax.ShapeDtypeStruct((ROWS_DEV, HEADS * HD), jnp.bfloat16),
        name="combine",
    )(parts)


def to_all(x, axes, count):
    return lax.all_to_all(jnp.broadcast_to(x[None], (count,) + x.shape), axes, 0, 0)


def shards(queries, prompt_kv, response_kv, logits, token_ids, lengths, rewards):
    z = lax.axis_index("z")
    spot = lax.axis_index(PLANE_AXES)
    depth = lax.axis_size("z")
    responses = lengths.shape[0]
    prompt_dev = prompt_kv.shape[0]

    kv_here = jnp.concatenate(
        [prompt_kv.reshape(prompt_dev, 2 * HD), response_kv.reshape(ROWS_DEV, 2 * HD)], axis=0
    )
    gathered = lax.all_gather(kv_here, "z", axis=0)
    q = lax.all_gather(queries.reshape(ROWS_DEV, HEADS * HD), PLANE_AXES, axis=0)

    vocab_base = (lax.axis_index("tp") * logits.shape[1]).astype(jnp.int32).reshape(1)
    stats = to_all(logit_stats(logits, token_ids, vocab_base), "tp", lax.axis_size("tp"))
    peaks, sums, picks = stats[:, 0], stats[:, 1], stats[:, 2]
    peak = jnp.max(peaks, axis=0)
    spread = jnp.sum(sums * jnp.exp(peaks - peak), axis=0)
    logprob = jnp.sum(picks, axis=0) - peak - jnp.log(spread)
    ends_at = jnp.cumsum(lengths)
    rows = (z * PLANE + spot) * ROWS_DEV + jnp.arange(ROWS_DEV, dtype=jnp.int32)
    segment = jnp.sum((rows[:, None] >= ends_at[None, :]).astype(jnp.int32), axis=1)
    token_logprob = jnp.where(segment < responses, logprob, 0.0)
    members = segment[:, None] == jnp.arange(128, dtype=jnp.int32)[None, :]
    part = jnp.sum(jnp.where(members, token_logprob[:, None], 0.0), axis=0)
    parts = to_all(part[None], CTX, depth * PLANE)
    response_sum = jnp.sum(parts[:, 0], axis=0)[:responses]
    length_float = lengths.astype(jnp.float32)
    adjusted = rewards - 0.5 * length_float / 2048
    advantage = adjusted - jnp.mean(adjusted)
    response_objective = -advantage * response_sum / length_float

    prompt = gathered[:, :prompt_dev].reshape(depth * prompt_dev, 2 * HD)
    reach = 5
    low = jnp.maximum(z - (reach - 1), 0)
    own = lax.dynamic_slice_in_dim(gathered[:, prompt_dev:], low, reach, 0)
    own = own.reshape(reach * ROWS_DEV, 2 * HD)
    place = jnp.stack(
        [z * PLANE * ROWS_DEV, (low * PLANE + spot) * ROWS_DEV]
    ).astype(jnp.int32)
    partial = attend(lengths, place, q, prompt, own)
    exchanged = lax.all_to_all(partial, PLANE_AXES, 0, 0)
    context = combine(exchanged).reshape(ROWS_DEV, HEADS, HD)
    return (context, token_logprob, response_objective)


def solution(mesh):
    fine = Mesh(mesh.devices.reshape(16, 2, 2, 8), ("z", "yl", "core", "tp"))
    return jax.shard_map(
        shards,
        mesh=fine,
        in_specs=(
            P(CTX, "tp", None),
            P(CTX, None, "tp", None),
            P(CTX, None, "tp", None),
            P(CTX, "tp"),
            P(CTX),
            P(),
            P(),
        ),
        out_specs=(P(CTX, "tp", None), P(CTX), P()),
        check_vma=False,
    )
```

```python
import functools
import math

import jax
import jax.numpy as jnp
from jax import lax
from jax.experimental import pallas as pl
from jax.experimental.pallas import tpu as pltpu
from jax.sharding import Mesh, PartitionSpec as P

HD = 128
HEADS = 4
ROWS_DEV = 128
PLANE = 4
TILE = 256
SCALE = 1.0 / math.sqrt(HD)
LOG2E = 1.4426950408889634
Z = ("zh", "zl")
CTX = Z + ("yl", "core")
PLANE_AXES = ("yl", "core")
MIB = 1 << 20


def logit_kernel(token_ref, base_ref, logits_ref, out_ref, stat_ref):
    step = pl.program_id(0)
    rows = logits_ref.shape[0]
    width = logits_ref.shape[1]
    here = pl.ds(pl.multiple_of(step * rows, rows), rows)
    wide = logits_ref[...].astype(jnp.float32)
    peak = jnp.max(wide, axis=1, keepdims=True)
    total = jnp.sum(jnp.exp(wide - peak), axis=1, keepdims=True)
    target = token_ref[...] - base_ref[0]
    columns = lax.broadcasted_iota(jnp.int32, (rows, width), 1)
    picked = jnp.sum(jnp.where(columns == target, wide, 0.0), axis=1, keepdims=True)
    lane = lax.broadcasted_iota(jnp.int32, (rows, 128), 1)
    stat_ref[here, :] = jnp.where(
        lane == 0, peak, jnp.where(lane == 1, total, picked)
    )

    @pl.when(step == pl.num_programs(0) - 1)
    def _():
        out_ref[...] = stat_ref[...].T[:8]


def logit_stats(logits, token_ids, vocab_base):
    rows, width = logits.shape
    block = 32
    return pl.pallas_call(
        logit_kernel,
        grid=(rows // block,),
        in_specs=[
            pl.BlockSpec((block, 1), lambda i: (i, 0)),
            pl.BlockSpec(memory_space=pltpu.SMEM),
            pl.BlockSpec((block, width), lambda i: (i, 0)),
        ],
        out_specs=pl.BlockSpec((8, 128), lambda i: (0, 0)),
        out_shape=jax.ShapeDtypeStruct((8, 128), jnp.float32),
        scratch_shapes=[pltpu.VMEM((rows, 128), jnp.float32)],
        compiler_params=pltpu.CompilerParams(vmem_limit_bytes=32 * MIB),
        cost_estimate=pl.CostEstimate(
            flops=8 * rows * width, bytes_accessed=2 * rows * width, transcendentals=rows * width
        ),
        name="logit_stats",
    )(token_ids.reshape(rows, 1), vocab_base, logits)


def nt(a, b):
    return lax.dot_general(a, b, (((1,), (1,)), ((), ())), preferred_element_type=jnp.float32)


def attend_kernel(pieces, first, last, *refs):
    lengths_ref, place_ref, q_ref = refs[:3]
    count = len(pieces)
    kv_refs = refs[3 : 3 + count]
    refs = refs[3 + count :]
    if not first:
        acc_in, stat_in = refs[:2]
        refs = refs[2:]
    if last:
        out_ref = refs[0]
        refs = refs[1:]
    else:
        acc_out, stat_out = refs[:2]
        refs = refs[2:]
    v_refs = refs
    for kv_ref, v_ref in zip(kv_refs, v_refs):
        v_ref[:, :HD] = kv_ref[:, HD:]
        v_ref[:, HD:] = jnp.ones((kv_ref.shape[0], HD), jnp.bfloat16)
    lane = lax.broadcasted_iota(jnp.int32, (TILE, HD), 1)
    per = TILE // ROWS_DEV

    def row_tile(t, carry):
        rows = place_ref[0] + t * TILE + lax.broadcasted_iota(jnp.int32, (TILE, 1), 0)
        start = jnp.zeros((TILE, 1), jnp.int32)
        edge = jnp.int32(0)
        for r in range(lengths_ref.shape[0]):
            edge = edge + lengths_ref[r]
            start = jnp.where(rows >= edge, edge, start)
        start = jnp.where(rows >= edge, rows, start)
        devs = pl.ds(t * per, per)
        packed = jnp.zeros((TILE, HD), jnp.float32)
        if not first:
            stat = stat_in[devs].reshape(TILE, HD)
        for h in range(HEADS):
            lanes = slice(h * HD, (h + 1) * HD)
            q = q_ref[devs, :, lanes].reshape(TILE, HD)
            tops = [] if first else [stat[:, h : h + 1]]
            scores = []
            answer = 0
            for kv_ref, v_ref, spans in zip(kv_refs, v_refs, pieces):
                for low, high, masked in spans:
                    s = nt(q, kv_ref[low:high, :HD])
                    if masked:
                        answer += 1
                        keys = place_ref[answer] + lax.broadcasted_iota(
                            jnp.int32, (TILE, high - low), 1
                        )
                        s = jnp.where((keys >= start) & (keys <= rows), s, -1e30)
                    tops.append(jnp.max(s, axis=1, keepdims=True))
                    scores.append((s, v_ref, low, high))
            m = tops[0]
            for top in tops[1:]:
                m = jnp.maximum(m, top)
            acc = 0.0
            for s, v_ref, low, high in scores:
                p = jnp.exp2((s - m) * (SCALE * LOG2E)).astype(jnp.bfloat16)
                acc = acc + jnp.dot(p, v_ref[low:high, :], preferred_element_type=jnp.float32)
            weighted, denominator = acc[:, :HD], acc[:, HD:]
            if not first:
                shrink = jnp.exp2((tops[0] - m) * (SCALE * LOG2E))
                weighted = weighted + shrink * acc_in[devs, :, lanes].reshape(TILE, HD)
                denominator = denominator + shrink * stat[:, HEADS + h : HEADS + h + 1]
            if last:
                out_ref[devs, :, lanes] = (
                    (weighted / denominator).astype(jnp.bfloat16).reshape(per, ROWS_DEV, HD)
                )
                lse = m * SCALE + jnp.log(denominator)
                high_part = lse.astype(jnp.bfloat16).astype(jnp.float32)
                middle = (lse - high_part).astype(jnp.bfloat16).astype(jnp.float32)
                low_part = lse - high_part - middle
                packed = jnp.where(lane == 3 * h, high_part, packed)
                packed = jnp.where(lane == 3 * h + 1, middle, packed)
                packed = jnp.where(lane == 3 * h + 2, low_part, packed)
            else:
                acc_out[devs, :, lanes] = weighted.reshape(per, ROWS_DEV, HD)
                packed = jnp.where(lane == h, m, packed)
                packed = jnp.where(lane == HEADS + h, denominator, packed)
        if last:
            out_ref[devs, :, HEADS * HD :] = packed.astype(jnp.bfloat16).reshape(
                per, ROWS_DEV, HD
            )
        else:
            stat_out[devs] = packed.reshape(per, ROWS_DEV, HD)
        return carry

    lax.fori_loop(0, PLANE * ROWS_DEV // TILE, row_tile, 0)


def attend(lengths, place, q, blocks, pieces, state, last):
    vmem = pl.BlockSpec(memory_space=pltpu.VMEM)
    smem = pl.BlockSpec(memory_space=pltpu.SMEM)
    keys = sum(high - low for spans in pieces for low, high, masked in spans)
    pairs = PLANE * ROWS_DEV * HEADS * keys
    if last:
        out_shape = jax.ShapeDtypeStruct((PLANE, ROWS_DEV, HEADS * HD + HD), jnp.bfloat16)
        out_specs = vmem
    else:
        out_shape = (
            jax.ShapeDtypeStruct((PLANE, ROWS_DEV, HEADS * HD), jnp.float32),
            jax.ShapeDtypeStruct((PLANE, ROWS_DEV, HD), jnp.float32),
        )
        out_specs = (vmem, vmem)
    return pl.pallas_call(
        functools.partial(attend_kernel, pieces, not state, last),
        in_specs=[smem, smem] + [vmem] * (1 + len(blocks) + len(state)),
        out_specs=out_specs,
        out_shape=out_shape,
        scratch_shapes=[pltpu.VMEM((block.shape[0], 2 * HD), jnp.bfloat16) for block in blocks],
        compiler_params=pltpu.CompilerParams(vmem_limit_bytes=40 * MIB),
        cost_estimate=pl.CostEstimate(
            flops=8 * HD * pairs, bytes_accessed=512 * keys + 2 * MIB, transcendentals=pairs
        ),
        name="attend",
    )(lengths, place, q, *blocks, *state)


def combine_kernel(parts_ref, out_ref):
    for h in range(HEADS):
        lanes = slice(h * HD, (h + 1) * HD)
        lse = []
        for j in range(PLANE):
            base = HEADS * HD + 3 * h
            bits = parts_ref[j, :, HEADS * HD :].astype(jnp.float32)
            lse.append(
                bits[:, 3 * h : 3 * h + 1] + bits[:, 3 * h + 1 : 3 * h + 2] + bits[:, 3 * h + 2 : 3 * h + 3]
            )
        top = jnp.maximum(jnp.maximum(lse[0], lse[1]), jnp.maximum(lse[2], lse[3]))
        weights = [jnp.exp(x - top) for x in lse]
        share = 1.0 / (weights[0] + weights[1] + weights[2] + weights[3])
        total = sum(
            (weights[j] * share) * parts_ref[j, :, lanes].astype(jnp.float32) for j in range(PLANE)
        )
        out_ref[:, lanes] = total.astype(jnp.bfloat16)


def combine(parts):
    vmem = pl.BlockSpec(memory_space=pltpu.VMEM)
    return pl.pallas_call(
        combine_kernel,
        in_specs=[vmem],
        out_specs=vmem,
        out_shape=jax.ShapeDtypeStruct((ROWS_DEV, HEADS * HD), jnp.bfloat16),
        name="combine",
    )(parts)


def to_all(x, axes, count):
    return lax.all_to_all(jnp.broadcast_to(x[None], (count,) + x.shape), axes, 0, 0)


def shift(x, distance):
    depth = lax.axis_size("zh") * lax.axis_size("zl")
    return lax.ppermute(x, Z, [(i, (i + distance) % depth) for i in range(depth)])


def shards(queries, prompt_kv, response_kv, logits, token_ids, lengths, rewards):
    z = lax.axis_index(Z)
    spot = lax.axis_index(PLANE_AXES)
    depth = lax.axis_size("zh") * lax.axis_size("zl")
    responses = lengths.shape[0]
    pb = prompt_kv.shape[0]
    rb = response_kv.shape[0]

    own = jnp.concatenate(
        [prompt_kv.reshape(pb, 2 * HD), response_kv.reshape(rb, 2 * HD)], axis=0
    )
    plus4 = shift(own, 4)
    minus4 = shift(own[:pb], -4)
    q = lax.all_gather(queries.reshape(ROWS_DEV, HEADS * HD), PLANE_AXES, axis=0)
    eight_a = shift(minus4[: pb // 2], -4)
    eight_b = shift(plus4[pb // 2 : pb], 4)

    vocab_base = (lax.axis_index("tp") * logits.shape[1]).astype(jnp.int32).reshape(1)
    stats = to_all(logit_stats(logits, token_ids, vocab_base), "tp", lax.axis_size("tp"))
    peaks, sums, picks = stats[:, 0], stats[:, 1], stats[:, 2]
    peak = jnp.max(peaks, axis=0)
    spread = jnp.sum(sums * jnp.exp(peaks - peak), axis=0)
    logprob = jnp.sum(picks, axis=0) - peak - jnp.log(spread)
    ends_at = jnp.cumsum(lengths)
    rows = (z * PLANE + spot) * ROWS_DEV + jnp.arange(ROWS_DEV, dtype=jnp.int32)
    segment = jnp.sum((rows[:, None] >= ends_at[None, :]).astype(jnp.int32), axis=1)
    token_logprob = jnp.where(segment < responses, logprob, 0.0)
    members = segment[:, None] == jnp.arange(128, dtype=jnp.int32)[None, :]
    part = jnp.sum(jnp.where(members, token_logprob[:, None], 0.0), axis=0)
    part = jnp.sum(to_all(part[None], ("zl",) + PLANE_AXES, 8)[:, 0], axis=0)
    part = jnp.sum(to_all(part[None], "zh", 8)[:, 0], axis=0)
    response_sum = part[:responses]
    length_float = lengths.astype(jnp.float32)
    adjusted = rewards - 0.5 * length_float / 2048
    advantage = adjusted - jnp.mean(adjusted)
    response_objective = -advantage * response_sum / length_float

    def place(*planes):
        first_keys = [((p + depth) % depth * PLANE + spot) * rb for p in planes]
        return jnp.stack([z * PLANE * ROWS_DEV] + first_keys).astype(jnp.int32)

    send_right = jnp.concatenate(
        [own[:pb], plus4[:pb], own[pb:], minus4, eight_a, eight_b], axis=0
    )
    send_left = jnp.concatenate(
        [own[:pb], minus4, plus4[pb:], plus4[:pb], eight_a, eight_b], axis=0
    )
    right = shift(send_right, 1)
    left = shift(send_left, -1)
    whole = ((0, 2 * pb, False), (2 * pb, 2 * pb + rb, True), (2 * pb + rb, 4 * pb + rb, False))
    state = attend(
        lengths, place(z, z - 4), q, [send_right, plus4], [whole, ((pb, pb + rb, True),)], (), False
    )
    right2 = shift(right[: 2 * pb + rb], 1)
    left2 = shift(left[: 2 * pb], -1)
    state = attend(
        lengths, place(z - 1, z - 3), q, [right, left], [whole, whole], state, False
    )
    partial = attend(
        lengths, place(z - 2), q, [right2, left2], [whole[:2], whole[:1]], state, True
    )
    exchanged = lax.all_to_all(partial, PLANE_AXES, 0, 0)
    context = combine(exchanged).reshape(ROWS_DEV, HEADS, HD)
    return (context, token_logprob, response_objective)


def solution(mesh):
    fine = Mesh(mesh.devices.reshape(8, 2, 2, 2, 8), ("zh", "zl", "yl", "core", "tp"))
    return jax.shard_map(
        shards,
        mesh=fine,
        in_specs=(
            P(CTX, "tp", None),
            P(CTX, None, "tp", None),
            P(CTX, None, "tp", None),
            P(CTX, "tp"),
            P(CTX),
            P(),
            P(),
        ),
        out_specs=(P(CTX, "tp", None), P(CTX), P()),
        check_vma=False,
    )
```

```python
import functools
import math

import jax
import jax.numpy as jnp
from jax import lax
from jax.experimental import pallas as pl
from jax.experimental.pallas import tpu as pltpu
from jax.sharding import Mesh, PartitionSpec as P

HD = 128
HEADS = 4
ROWS_DEV = 128
PLANE = 4
TILE = 512
SCALE = 1.0 / math.sqrt(HD)
LOG2E = 1.4426950408889634
Z = ("zh", "zl")
CTX = Z + ("yl", "core")
PLANE_AXES = ("yl", "core")
MIB = 1 << 20


def logit_kernel(token_ref, base_ref, logits_ref, out_ref, stat_ref, target_ref):
    step = pl.program_id(0)
    rows, width = logits_ref.shape

    @pl.when(step == 0)
    def _():
        wanted = jnp.broadcast_to(token_ref[...].astype(jnp.float32), target_ref.shape)
        target_ref[...] = wanted.T.astype(jnp.int32) - base_ref[0]

    here = pl.ds(pl.multiple_of(step * rows, rows), rows)
    wide = logits_ref[...].astype(jnp.float32)
    peak = jnp.max(wide, axis=1, keepdims=True)
    total = jnp.sum(jnp.exp(wide - peak), axis=1, keepdims=True)
    columns = lax.broadcasted_iota(jnp.int32, (rows, width), 1)
    matches = columns == target_ref[here, :1]
    picked = jnp.sum(jnp.where(matches, wide, 0.0), axis=1, keepdims=True)
    lane = lax.broadcasted_iota(jnp.int32, (rows, 128), 1)
    stat_ref[here, :] = jnp.where(
        lane == 0, peak, jnp.where(lane == 1, total, picked)
    )

    @pl.when(step == pl.num_programs(0) - 1)
    def _():
        out_ref[...] = jnp.broadcast_to(stat_ref[...].T[None, :8], out_ref.shape)


def logit_stats(logits, token_ids, vocab_base, copies):
    rows, width = logits.shape
    block = 32
    return pl.pallas_call(
        logit_kernel,
        grid=(rows // block,),
        in_specs=[
            pl.BlockSpec((1, rows), lambda i: (0, 0)),
            pl.BlockSpec(memory_space=pltpu.SMEM),
            pl.BlockSpec((block, width), lambda i: (i, 0)),
        ],
        out_specs=pl.BlockSpec((copies, 8, rows), lambda i: (0, 0, 0)),
        out_shape=jax.ShapeDtypeStruct((copies, 8, rows), jnp.float32),
        scratch_shapes=[pltpu.VMEM((rows, 128), jnp.float32), pltpu.VMEM((rows, 128), jnp.int32)],
        compiler_params=pltpu.CompilerParams(vmem_limit_bytes=32 * MIB),
        cost_estimate=pl.CostEstimate(
            flops=8 * rows * width, bytes_accessed=2 * rows * width, transcendentals=rows * width
        ),
        name="logit_stats",
    )(token_ids.reshape(1, rows), vocab_base, logits)


def nt(a, b):
    return lax.dot_general(a, b, (((1,), (1,)), ((), ())), preferred_element_type=jnp.float32)


def attend_kernel(pieces, first, last, *refs):
    lengths_ref, place_ref, q_ref = refs[:3]
    count = len(pieces)
    kv_refs = refs[3 : 3 + count]
    refs = refs[3 + count :]
    if not first:
        acc_in, stat_in = refs[:2]
        refs = refs[2:]
    if last:
        out_ref = refs[0]
        refs = refs[1:]
    else:
        acc_out, stat_out = refs[:2]
        refs = refs[2:]
    v_refs = refs
    for kv_ref, v_ref in zip(kv_refs, v_refs):
        v_ref[:, :HD] = kv_ref[:, HD:]
        v_ref[:, HD:] = jnp.ones((kv_ref.shape[0], HD), jnp.bfloat16)
    lane = lax.broadcasted_iota(jnp.int32, (TILE, HD), 1)
    per = TILE // ROWS_DEV

    def row_tile(t, carry):
        rows = place_ref[0] + t * TILE + lax.broadcasted_iota(jnp.int32, (TILE, 1), 0)
        start = jnp.zeros((TILE, 1), jnp.int32)
        edge = jnp.int32(0)
        for r in range(lengths_ref.shape[0]):
            edge = edge + lengths_ref[r]
            start = jnp.where(rows >= edge, edge, start)
        start = jnp.where(rows >= edge, rows, start)
        devs = pl.ds(t * per, per)
        packed = jnp.zeros((TILE, HD), jnp.float32)
        if not first:
            stat = stat_in[devs].reshape(TILE, HD)
        for h in range(HEADS):
            lanes = slice(h * HD, (h + 1) * HD)
            q = q_ref[devs, :, lanes].reshape(TILE, HD)
            tops = [] if first else [stat[:, h : h + 1]]
            scores = []
            answer = 0
            for kv_ref, v_ref, spans in zip(kv_refs, v_refs, pieces):
                for low, high, masked in spans:
                    s = nt(q, kv_ref[low:high, :HD])
                    if masked:
                        answer += 1
                        keys = place_ref[answer] + lax.broadcasted_iota(
                            jnp.int32, (TILE, high - low), 1
                        )
                        s = jnp.where((keys >= start) & (keys <= rows), s, -1e30)
                    tops.append(jnp.max(s, axis=1, keepdims=True))
                    scores.append((s, v_ref, low, high))
            m = tops[0]
            for top in tops[1:]:
                m = jnp.maximum(m, top)
            acc = 0.0
            for s, v_ref, low, high in scores:
                p = jnp.exp2((s - m) * (SCALE * LOG2E)).astype(jnp.bfloat16)
                acc = acc + jnp.dot(p, v_ref[low:high, :], preferred_element_type=jnp.float32)
            weighted, denominator = acc[:, :HD], acc[:, HD:]
            if not first:
                shrink = jnp.exp2((tops[0] - m) * (SCALE * LOG2E))
                weighted = weighted + shrink * acc_in[devs, :, lanes].reshape(TILE, HD)
                denominator = denominator + shrink * stat[:, HEADS + h : HEADS + h + 1]
            if last:
                out_ref[devs, :, lanes] = (
                    (weighted / denominator).astype(jnp.bfloat16).reshape(per, ROWS_DEV, HD)
                )
                lse = m * SCALE + jnp.log(denominator)
                high_part = lse.astype(jnp.bfloat16).astype(jnp.float32)
                middle = (lse - high_part).astype(jnp.bfloat16).astype(jnp.float32)
                low_part = lse - high_part - middle
                packed = jnp.where(lane == 3 * h, high_part, packed)
                packed = jnp.where(lane == 3 * h + 1, middle, packed)
                packed = jnp.where(lane == 3 * h + 2, low_part, packed)
            else:
                acc_out[devs, :, lanes] = weighted.reshape(per, ROWS_DEV, HD)
                packed = jnp.where(lane == h, m, packed)
                packed = jnp.where(lane == HEADS + h, denominator, packed)
        if last:
            out_ref[devs, :, HEADS * HD :] = packed.astype(jnp.bfloat16).reshape(
                per, ROWS_DEV, HD
            )
        else:
            stat_out[devs] = packed.reshape(per, ROWS_DEV, HD)
        return carry

    lax.fori_loop(0, PLANE * ROWS_DEV // TILE, row_tile, 0)


def attend(lengths, place, q, blocks, pieces, state, last):
    vmem = pl.BlockSpec(memory_space=pltpu.VMEM)
    smem = pl.BlockSpec(memory_space=pltpu.SMEM)
    keys = sum(high - low for spans in pieces for low, high, masked in spans)
    pairs = PLANE * ROWS_DEV * HEADS * keys
    if last:
        out_shape = jax.ShapeDtypeStruct((PLANE, ROWS_DEV, HEADS * HD + HD), jnp.bfloat16)
        out_specs = vmem
    else:
        out_shape = (
            jax.ShapeDtypeStruct((PLANE, ROWS_DEV, HEADS * HD), jnp.float32),
            jax.ShapeDtypeStruct((PLANE, ROWS_DEV, HD), jnp.float32),
        )
        out_specs = (vmem, vmem)
    return pl.pallas_call(
        functools.partial(attend_kernel, pieces, not state, last),
        in_specs=[smem, smem] + [vmem] * (1 + len(blocks) + len(state)),
        out_specs=out_specs,
        out_shape=out_shape,
        scratch_shapes=[pltpu.VMEM((block.shape[0], 2 * HD), jnp.bfloat16) for block in blocks],
        compiler_params=pltpu.CompilerParams(vmem_limit_bytes=40 * MIB),
        cost_estimate=pl.CostEstimate(
            flops=8 * HD * pairs, bytes_accessed=512 * keys + 2 * MIB, transcendentals=pairs
        ),
        name="attend",
    )(lengths, place, q, *blocks, *state)


def combine_kernel(parts_ref, out_ref):
    tops = []
    for j in range(PLANE):
        bits = parts_ref[j, :, HEADS * HD :].astype(jnp.float32)
        tops.append(bits + pltpu.roll(bits, HD - 1, 1) + pltpu.roll(bits, HD - 2, 1))
    top = jnp.maximum(jnp.maximum(tops[0], tops[1]), jnp.maximum(tops[2], tops[3]))
    weights = [jnp.exp(x - top) for x in tops]
    share = 1.0 / (weights[0] + weights[1] + weights[2] + weights[3])
    weights = [x * share for x in weights]
    heads = []
    for h in range(HEADS):
        lanes = slice(h * HD, (h + 1) * HD)
        heads.append(
            sum(
                weights[j][:, 3 * h : 3 * h + 1] * parts_ref[j, :, lanes].astype(jnp.float32)
                for j in range(PLANE)
            )
        )
    out_ref[...] = jnp.stack(heads, axis=1).astype(jnp.bfloat16)


def combine(parts):
    rows = 32
    return pl.pallas_call(
        combine_kernel,
        grid=(ROWS_DEV // rows,),
        in_specs=[pl.BlockSpec((PLANE, rows, HEADS * HD + HD), lambda i: (0, i, 0))],
        out_specs=pl.BlockSpec((rows, HEADS, HD), lambda i: (i, 0, 0)),
        out_shape=jax.ShapeDtypeStruct((ROWS_DEV, HEADS, HD), jnp.bfloat16),
        name="combine",
    )(parts)


def to_all(x, axes, count):
    return lax.all_to_all(jnp.broadcast_to(x[None], (count,) + x.shape), axes, 0, 0)


def shift(x, distance):
    depth = lax.axis_size("zh") * lax.axis_size("zl")
    return lax.ppermute(x, Z, [(i, (i + distance) % depth) for i in range(depth)])


def shards(queries, prompt_kv, response_kv, logits, token_ids, lengths, rewards):
    z = lax.axis_index(Z)
    spot = lax.axis_index(PLANE_AXES)
    depth = lax.axis_size("zh") * lax.axis_size("zl")
    responses = lengths.shape[0]
    pb = prompt_kv.shape[0]
    rb = response_kv.shape[0]

    own = jnp.concatenate(
        [prompt_kv.reshape(pb, 2 * HD), response_kv.reshape(rb, 2 * HD)], axis=0
    )
    plus4 = shift(own, 4)
    minus4 = shift(own[:pb], -4)
    q = to_all(queries.reshape(ROWS_DEV, HEADS * HD), PLANE_AXES, PLANE)

    vocab_base = (lax.axis_index("tp") * logits.shape[1]).astype(jnp.int32).reshape(1)
    stats = logit_stats(logits, token_ids, vocab_base, lax.axis_size("tp"))
    stats, q = lax.optimization_barrier((stats, q))
    stats = lax.all_to_all(stats, "tp", 0, 0)
    def place(*planes):
        first_keys = [((p + depth) % depth * PLANE + spot) * rb for p in planes]
        return jnp.stack([z * PLANE * ROWS_DEV] + first_keys).astype(jnp.int32)

    send_right = jnp.concatenate([own[:pb], plus4[:pb], own[pb:], minus4], axis=0)
    send_left = jnp.concatenate([own[:pb], minus4, plus4[pb:], plus4[:pb]], axis=0)
    stats, *_ = lax.optimization_barrier((stats, send_right, send_left))
    right = shift(send_right, 1)
    left = shift(send_left, -1)
    half_a, half_b, *_ = lax.optimization_barrier(
        (minus4[: pb // 2], plus4[pb // 2 : pb], send_right, send_left)
    )
    eight_a = shift(half_a, -4)
    eight_b = shift(half_b, 4)
    peaks, sums, picks = stats[:, 0], stats[:, 1], stats[:, 2]
    peak = jnp.max(peaks, axis=0)
    spread = jnp.sum(sums * jnp.exp(peaks - peak), axis=0)
    logprob = jnp.sum(picks, axis=0) - peak - jnp.log(spread)
    ends_at = jnp.cumsum(lengths)
    rows = (z * PLANE + spot) * ROWS_DEV + jnp.arange(ROWS_DEV, dtype=jnp.int32)
    segment = jnp.sum((rows[:, None] >= ends_at[None, :]).astype(jnp.int32), axis=1)
    token_logprob = jnp.where(segment < responses, logprob, 0.0)
    members = segment[:, None] == jnp.arange(128, dtype=jnp.int32)[None, :]
    part = jnp.sum(jnp.where(members, token_logprob[:, None], 0.0), axis=0)
    part = jnp.sum(to_all(part[None], ("zl",) + PLANE_AXES, 8)[:, 0], axis=0)

    whole = ((0, 2 * pb, False), (2 * pb, 2 * pb + rb, True), (2 * pb + rb, 3 * pb + rb, False))
    state = attend(
        lengths, place(z, z - 4), q, [send_right, plus4], [whole, ((pb, pb + rb, True),)], (), False
    )
    part, _ = lax.optimization_barrier((part, state[1]))
    eight = jnp.concatenate([eight_a, eight_b], axis=0)
    right2 = shift(jnp.concatenate([right[: 2 * pb + rb], eight], axis=0), 1)
    left2 = shift(jnp.concatenate([left[: 2 * pb], eight], axis=0), -1)
    part = jnp.sum(to_all(part[None], "zh", 8)[:, 0], axis=0)
    state = attend(
        lengths,
        place(z - 1, z - 3),
        q,
        [right, left, eight],
        [whole, whole, ((0, pb, False),)],
        state,
        False,
    )
    partial = attend(
        lengths, place(z - 2), q, [right2, left2], [whole, ((0, 3 * pb, False),)], state, True
    )
    exchanged = lax.all_to_all(partial, PLANE_AXES, 0, 0)
    context = combine(exchanged)

    response_sum = part[:responses]
    length_float = lengths.astype(jnp.float32)
    adjusted = rewards - 0.5 * length_float / 2048
    advantage = adjusted - jnp.mean(adjusted)
    response_objective = -advantage * response_sum / length_float

    return (context, token_logprob, response_objective)


def solution(mesh):
    fine = Mesh(mesh.devices.reshape(8, 2, 2, 2, 8), ("zh", "zl", "yl", "core", "tp"))
    return jax.shard_map(
        shards,
        mesh=fine,
        in_specs=(
            P(CTX, "tp", None),
            P(CTX, None, "tp", None),
            P(CTX, None, "tp", None),
            P(CTX, "tp"),
            P(CTX),
            P(),
            P(),
        ),
        out_specs=(P(CTX, "tp", None), P(CTX), P()),
        check_vma=False,
    )
```

```python
import functools
import math

import jax
import jax.numpy as jnp
from jax import lax
from jax.experimental import pallas as pl
from jax.experimental.pallas import tpu as pltpu
from jax.sharding import Mesh, PartitionSpec as P

HD = 128
HEADS = 4
ROWS_DEV = 128
PLANE = 4
TILE = 512
SCALE = 1.0 / math.sqrt(HD)
LOG2E = 1.4426950408889634
Z = ("zh", "zl")
CTX = Z + ("yl", "core")
SHARE = ("zl", "yl")
MIB = 1 << 20


def logit_kernel(token_ref, base_ref, logits_ref, out_ref, stat_ref, target_ref):
    step = pl.program_id(0)
    rows, width = logits_ref.shape

    @pl.when(step == 0)
    def _():
        wanted = jnp.broadcast_to(token_ref[...].astype(jnp.float32), target_ref.shape)
        target_ref[...] = wanted.T.astype(jnp.int32) - base_ref[0]

    here = pl.ds(pl.multiple_of(step * rows, rows), rows)
    wide = logits_ref[...].astype(jnp.float32)
    peak = jnp.max(wide, axis=1, keepdims=True)
    total = jnp.sum(jnp.exp(wide - peak), axis=1, keepdims=True)
    columns = lax.broadcasted_iota(jnp.int32, (rows, width), 1)
    matches = columns == target_ref[here, :1]
    picked = jnp.sum(jnp.where(matches, wide, 0.0), axis=1, keepdims=True)
    lane = lax.broadcasted_iota(jnp.int32, (rows, 128), 1)
    stat_ref[here, :] = jnp.where(
        lane == 0, peak, jnp.where(lane == 1, total, picked)
    )

    @pl.when(step == pl.num_programs(0) - 1)
    def _():
        out_ref[...] = jnp.broadcast_to(stat_ref[...].T[None, :8], out_ref.shape)


def logit_stats(logits, token_ids, vocab_base, copies):
    rows, width = logits.shape
    block = 32
    return pl.pallas_call(
        logit_kernel,
        grid=(rows // block,),
        in_specs=[
            pl.BlockSpec((1, rows), lambda i: (0, 0)),
            pl.BlockSpec(memory_space=pltpu.SMEM),
            pl.BlockSpec((block, width), lambda i: (i, 0)),
        ],
        out_specs=pl.BlockSpec((copies, 8, rows), lambda i: (0, 0, 0)),
        out_shape=jax.ShapeDtypeStruct((copies, 8, rows), jnp.float32),
        scratch_shapes=[pltpu.VMEM((rows, 128), jnp.float32), pltpu.VMEM((rows, 128), jnp.int32)],
        compiler_params=pltpu.CompilerParams(vmem_limit_bytes=32 * MIB),
        cost_estimate=pl.CostEstimate(
            flops=8 * rows * width, bytes_accessed=2 * rows * width, transcendentals=rows * width
        ),
        name="logit_stats",
    )(token_ids.reshape(1, rows), vocab_base, logits)


def nt(a, b):
    return lax.dot_general(a, b, (((1,), (1,)), ((), ())), preferred_element_type=jnp.float32)


def attend_kernel(pieces, first, last, *refs):
    lengths_ref, place_ref, q_ref = refs[:3]
    count = len(pieces)
    kv_refs = refs[3 : 3 + count]
    refs = refs[3 + count :]
    if not first:
        acc_in, stat_in = refs[:2]
        refs = refs[2:]
    if last:
        out_ref = refs[0]
        refs = refs[1:]
    else:
        acc_out, stat_out = refs[:2]
        refs = refs[2:]
    v_refs = refs
    for kv_ref, v_ref in zip(kv_refs, v_refs):
        v_ref[:, :HD] = kv_ref[:, HD:]
        v_ref[:, HD:] = jnp.ones((kv_ref.shape[0], HD), jnp.bfloat16)
    lane = lax.broadcasted_iota(jnp.int32, (TILE, HD), 1)
    per = TILE // ROWS_DEV

    def row_tile(t, carry):
        index = t * TILE + lax.broadcasted_iota(jnp.int32, (TILE, 1), 0)
        planes, spots = index // (2 * ROWS_DEV), index // ROWS_DEV % 2
        rows = place_ref[0] + (planes * PLANE + spots * 2) * ROWS_DEV + index % ROWS_DEV
        start = jnp.zeros((TILE, 1), jnp.int32)
        edge = jnp.int32(0)
        for r in range(lengths_ref.shape[0]):
            edge = edge + lengths_ref[r]
            start = jnp.where(rows >= edge, edge, start)
        start = jnp.where(rows >= edge, rows, start)
        devs = pl.ds(t * per, per)
        packed = jnp.zeros((TILE, HD), jnp.float32)
        if not first:
            stat = stat_in[devs].reshape(TILE, HD)
        for h in range(HEADS):
            lanes = slice(h * HD, (h + 1) * HD)
            q = q_ref[devs, :, lanes].reshape(TILE, HD)
            tops = [] if first else [stat[:, h : h + 1]]
            scores = []
            answer = 0
            for kv_ref, v_ref, spans in zip(kv_refs, v_refs, pieces):
                for low, high, masked in spans:
                    s = nt(q, kv_ref[low:high, :HD])
                    if masked:
                        answer += 1
                        column = lax.broadcasted_iota(jnp.int32, (TILE, high - low), 1)
                        keys = place_ref[answer] + column % ROWS_DEV
                        keys = keys - column // ROWS_DEV * (2 * PLANE * ROWS_DEV)
                        s = jnp.where((keys >= start) & (keys <= rows), s, -1e30)
                    tops.append(jnp.max(s, axis=1, keepdims=True))
                    scores.append((s, v_ref, low, high))
            m = tops[0]
            for top in tops[1:]:
                m = jnp.maximum(m, top)
            acc = 0.0
            for s, v_ref, low, high in scores:
                p = jnp.exp2((s - m) * (SCALE * LOG2E)).astype(jnp.bfloat16)
                acc = acc + jnp.dot(p, v_ref[low:high, :], preferred_element_type=jnp.float32)
            weighted, denominator = acc[:, :HD], acc[:, HD:]
            if not first:
                shrink = jnp.exp2((tops[0] - m) * (SCALE * LOG2E))
                weighted = weighted + shrink * acc_in[devs, :, lanes].reshape(TILE, HD)
                denominator = denominator + shrink * stat[:, HEADS + h : HEADS + h + 1]
            if last:
                out_ref[devs, :, lanes] = (
                    (weighted / denominator).astype(jnp.bfloat16).reshape(per, ROWS_DEV, HD)
                )
                lse = m * SCALE + jnp.log(denominator)
                high_part = lse.astype(jnp.bfloat16).astype(jnp.float32)
                middle = (lse - high_part).astype(jnp.bfloat16).astype(jnp.float32)
                low_part = lse - high_part - middle
                packed = jnp.where(lane == 3 * h, high_part, packed)
                packed = jnp.where(lane == 3 * h + 1, middle, packed)
                packed = jnp.where(lane == 3 * h + 2, low_part, packed)
            else:
                acc_out[devs, :, lanes] = weighted.reshape(per, ROWS_DEV, HD)
                packed = jnp.where(lane == h, m, packed)
                packed = jnp.where(lane == HEADS + h, denominator, packed)
        if last:
            out_ref[devs, :, HEADS * HD :] = packed.astype(jnp.bfloat16).reshape(
                per, ROWS_DEV, HD
            )
        else:
            stat_out[devs] = packed.reshape(per, ROWS_DEV, HD)
        return carry

    lax.fori_loop(0, PLANE * ROWS_DEV // TILE, row_tile, 0)


def attend(lengths, place, q, blocks, pieces, state, last):
    vmem = pl.BlockSpec(memory_space=pltpu.VMEM)
    smem = pl.BlockSpec(memory_space=pltpu.SMEM)
    keys = sum(high - low for spans in pieces for low, high, masked in spans)
    pairs = PLANE * ROWS_DEV * HEADS * keys
    if last:
        out_shape = jax.ShapeDtypeStruct((PLANE, ROWS_DEV, HEADS * HD + HD), jnp.bfloat16)
        out_specs = vmem
    else:
        out_shape = (
            jax.ShapeDtypeStruct((PLANE, ROWS_DEV, HEADS * HD), jnp.float32),
            jax.ShapeDtypeStruct((PLANE, ROWS_DEV, HD), jnp.float32),
        )
        out_specs = (vmem, vmem)
    return pl.pallas_call(
        functools.partial(attend_kernel, pieces, not state, last),
        in_specs=[smem, smem] + [vmem] * (1 + len(blocks) + len(state)),
        out_specs=out_specs,
        out_shape=out_shape,
        scratch_shapes=[pltpu.VMEM((block.shape[0], 2 * HD), jnp.bfloat16) for block in blocks],
        compiler_params=pltpu.CompilerParams(vmem_limit_bytes=40 * MIB),
        cost_estimate=pl.CostEstimate(
            flops=8 * HD * pairs, bytes_accessed=512 * keys + 2 * MIB, transcendentals=pairs
        ),
        name="attend",
    )(lengths, place, q, *blocks, *state)


def combine_kernel(parts_ref, out_ref):
    tops = []
    for j in range(PLANE):
        bits = parts_ref[j, :, HEADS * HD :].astype(jnp.float32)
        tops.append(bits + pltpu.roll(bits, HD - 1, 1) + pltpu.roll(bits, HD - 2, 1))
    top = jnp.maximum(jnp.maximum(tops[0], tops[1]), jnp.maximum(tops[2], tops[3]))
    weights = [jnp.exp(x - top) for x in tops]
    share = 1.0 / (weights[0] + weights[1] + weights[2] + weights[3])
    weights = [x * share for x in weights]
    heads = []
    for h in range(HEADS):
        lanes = slice(h * HD, (h + 1) * HD)
        heads.append(
            sum(
                weights[j][:, 3 * h : 3 * h + 1] * parts_ref[j, :, lanes].astype(jnp.float32)
                for j in range(PLANE)
            )
        )
    out_ref[...] = jnp.stack(heads, axis=1).astype(jnp.bfloat16)


def combine(parts):
    rows = 32
    return pl.pallas_call(
        combine_kernel,
        grid=(ROWS_DEV // rows,),
        in_specs=[pl.BlockSpec((PLANE, rows, HEADS * HD + HD), lambda i: (0, i, 0))],
        out_specs=pl.BlockSpec((rows, HEADS, HD), lambda i: (i, 0, 0)),
        out_shape=jax.ShapeDtypeStruct((ROWS_DEV, HEADS, HD), jnp.bfloat16),
        name="combine",
    )(parts)


def to_all(x, axes, count):
    return lax.all_to_all(jnp.broadcast_to(x[None], (count,) + x.shape), axes, 0, 0)


def shards(queries, prompt_kv, response_kv, logits, token_ids, lengths, rewards):
    pair = lax.axis_index("zh")
    z = lax.axis_index(Z)
    row = lax.axis_index("yl")
    core = lax.axis_index("core")
    pairs = lax.axis_size("zh")
    responses = lengths.shape[0]
    pb = prompt_kv.shape[0]
    rb = response_kv.shape[0]

    prompt = lax.all_gather(prompt_kv.reshape(pb, 2 * HD), ("zh", "core"), axis=0, tiled=True)
    q = lax.all_gather(queries.reshape(ROWS_DEV, HEADS * HD), SHARE, axis=0)

    vocab_base = (lax.axis_index("tp") * logits.shape[1]).astype(jnp.int32).reshape(1)
    stats = logit_stats(logits, token_ids, vocab_base, lax.axis_size("tp"))
    stats = lax.all_to_all(stats, "tp", 0, 0)

    own = response_kv.reshape(rb, 2 * HD)
    before = [
        lax.ppermute(own, "zh", [(i, (i + d) % pairs) for i in range(pairs)]) for d in (1, 2)
    ]
    mine = jnp.concatenate([own] + before, axis=0)
    other = lax.ppermute(mine, "core", [(0, 1), (1, 0)])

    peaks, sums, picks = stats[:, 0], stats[:, 1], stats[:, 2]
    peak = jnp.max(peaks, axis=0)
    spread = jnp.sum(sums * jnp.exp(peaks - peak), axis=0)
    logprob = jnp.sum(picks, axis=0) - peak - jnp.log(spread)
    ends_at = jnp.cumsum(lengths)
    block = z * PLANE + row * 2
    rows = (block + core) * ROWS_DEV + jnp.arange(ROWS_DEV, dtype=jnp.int32)
    segment = jnp.sum((rows[:, None] >= ends_at[None, :]).astype(jnp.int32), axis=1)
    token_logprob = jnp.where(segment < responses, logprob, 0.0)
    members = segment[:, None] == jnp.arange(128, dtype=jnp.int32)[None, :]
    part = jnp.sum(jnp.where(members, token_logprob[:, None], 0.0), axis=0)
    part = jnp.sum(to_all(part[None], CTX, 64)[:, 0], axis=0)
    response_sum = part[:responses]
    length_float = lengths.astype(jnp.float32)
    adjusted = rewards - 0.5 * length_float / 2048
    advantage = adjusted - jnp.mean(adjusted)
    response_objective = -advantage * response_sum / length_float

    first_row = (pair * 2 * PLANE + core) * ROWS_DEV
    place = jnp.stack(
        [first_row, (block + core) * ROWS_DEV, (block + 1 - core) * ROWS_DEV]
    ).astype(jnp.int32)
    masked = ((0, 3 * rb, True),)
    state = attend(lengths, place, q, [mine, other], [masked, masked], (), False)
    half = prompt.shape[0] // 2
    spans = ((0, half, False), (half, 2 * half, False))
    partial = attend(lengths, place, q, [prompt], [spans], state, True)
    exchanged = lax.all_to_all(partial, SHARE, 0, 0)
    context = combine(exchanged)
    return (context, token_logprob, response_objective)


def solution(mesh):
    fine = Mesh(mesh.devices.reshape(8, 2, 2, 2, 8), ("zh", "zl", "yl", "core", "tp"))
    return jax.shard_map(
        shards,
        mesh=fine,
        in_specs=(
            P(CTX, "tp", None),
            P(CTX, None, "tp", None),
            P(CTX, None, "tp", None),
            P(CTX, "tp"),
            P(CTX),
            P(),
            P(),
        ),
        out_specs=(P(CTX, "tp", None), P(CTX), P()),
        check_vma=False,
    )
```

```python
import functools
import math

import jax
import jax.numpy as jnp
from jax import lax
from jax.experimental import pallas as pl
from jax.experimental.pallas import tpu as pltpu
from jax.sharding import Mesh, PartitionSpec as P

HD = 128
HEADS = 4
ROWS_DEV = 128
PLANE = 4
TILE = 512
CHUNK = 512
SCALE = 1.0 / math.sqrt(HD)
LOG2E = 1.4426950408889634
Z = ("zh", "zl")
CTX = Z + ("yl", "core")
SHARE = ("zl", "yl")
MIB = 1 << 20


def logit_kernel(token_ref, base_ref, logits_ref, out_ref, stat_ref, target_ref):
    step = pl.program_id(0)
    rows, width = logits_ref.shape

    @pl.when(step == 0)
    def _():
        wanted = jnp.broadcast_to(token_ref[...].astype(jnp.float32), target_ref.shape)
        target_ref[...] = wanted.T.astype(jnp.int32) - base_ref[0]

    here = pl.ds(pl.multiple_of(step * rows, rows), rows)
    wide = logits_ref[...].astype(jnp.float32)
    peak = jnp.max(wide, axis=1, keepdims=True)
    total = jnp.sum(jnp.exp(wide - peak), axis=1, keepdims=True)
    columns = lax.broadcasted_iota(jnp.int32, (rows, width), 1)
    matches = columns == target_ref[here, :1]
    picked = jnp.sum(jnp.where(matches, wide, 0.0), axis=1, keepdims=True)
    lane = lax.broadcasted_iota(jnp.int32, (rows, 128), 1)
    stat_ref[here, :] = jnp.where(
        lane == 0, peak, jnp.where(lane == 1, total, picked)
    )

    @pl.when(step == pl.num_programs(0) - 1)
    def _():
        out_ref[...] = jnp.broadcast_to(stat_ref[...].T[None, :8], out_ref.shape)


def logit_stats(logits, token_ids, vocab_base, copies):
    rows, width = logits.shape
    block = 32
    return pl.pallas_call(
        logit_kernel,
        grid=(rows // block,),
        in_specs=[
            pl.BlockSpec((1, rows), lambda i: (0, 0)),
            pl.BlockSpec(memory_space=pltpu.SMEM),
            pl.BlockSpec((block, width), lambda i: (i, 0)),
        ],
        out_specs=pl.BlockSpec((copies, 8, rows), lambda i: (0, 0, 0)),
        out_shape=jax.ShapeDtypeStruct((copies, 8, rows), jnp.float32),
        scratch_shapes=[pltpu.VMEM((rows, 128), jnp.float32), pltpu.VMEM((rows, 128), jnp.int32)],
        compiler_params=pltpu.CompilerParams(vmem_limit_bytes=32 * MIB),
        cost_estimate=pl.CostEstimate(
            flops=8 * rows * width, bytes_accessed=2 * rows * width, transcendentals=rows * width
        ),
        name="logit_stats",
    )(token_ids.reshape(1, rows), vocab_base, logits)


def nt(a, b):
    return lax.dot_general(a, b, (((1,), (1,)), ((), ())), preferred_element_type=jnp.float32)


def attend_kernel(pieces, first, last, *refs):
    lengths_ref, place_ref, q_ref = refs[:3]
    count = len(pieces)
    kv_refs = refs[3 : 3 + count]
    refs = refs[3 + count :]
    if not first:
        acc_in, stat_in = refs[:2]
        refs = refs[2:]
    if last:
        out_ref = refs[0]
        refs = refs[1:]
    else:
        acc_out, stat_out = refs[:2]
        refs = refs[2:]
    v_refs = refs
    for kv_ref, v_ref in zip(kv_refs, v_refs):
        v_ref[:, :HD] = kv_ref[:, HD:]
        v_ref[:, HD:] = jnp.ones((kv_ref.shape[0], HD), jnp.bfloat16)
    lane = lax.broadcasted_iota(jnp.int32, (TILE, HD), 1)
    per = TILE // ROWS_DEV

    def row_tile(t, carry):
        index = t * TILE + lax.broadcasted_iota(jnp.int32, (TILE, 1), 0)
        planes, spots = index // (2 * ROWS_DEV), index // ROWS_DEV % 2
        rows = place_ref[0] + (planes * PLANE + spots * 2) * ROWS_DEV + index % ROWS_DEV
        start = jnp.zeros((TILE, 1), jnp.int32)
        edge = jnp.int32(0)
        for r in range(lengths_ref.shape[0]):
            edge = edge + lengths_ref[r]
            start = jnp.where(rows >= edge, edge, start)
        start = jnp.where(rows >= edge, rows, start)
        devs = pl.ds(t * per, per)
        packed = jnp.zeros((TILE, HD), jnp.float32)
        if not first:
            stat = stat_in[devs].reshape(TILE, HD)
        for h in range(HEADS):
            lanes = slice(h * HD, (h + 1) * HD)
            q = q_ref[devs, :, lanes].reshape(TILE, HD)
            tops = [] if first else [stat[:, h : h + 1]]
            scores = []
            answer = 0
            for kv_ref, v_ref, spans in zip(kv_refs, v_refs, pieces):
                for low, high, masked in spans:
                    s = nt(q, kv_ref[low:high, :HD])
                    if masked:
                        answer += 1
                        column = lax.broadcasted_iota(jnp.int32, (TILE, high - low), 1)
                        keys = place_ref[answer] + column % ROWS_DEV
                        keys = keys - column // ROWS_DEV * (2 * PLANE * ROWS_DEV)
                        s = jnp.where((keys >= start) & (keys <= rows), s, -1e30)
                    tops.append(jnp.max(s, axis=1, keepdims=True))
                    scores.append((s, v_ref, low, high))
            m = tops[0]
            for top in tops[1:]:
                m = jnp.maximum(m, top)
            acc = 0.0
            for s, v_ref, low, high in scores:
                p = jnp.exp2((s - m) * (SCALE * LOG2E)).astype(jnp.bfloat16)
                acc = acc + jnp.dot(p, v_ref[low:high, :], preferred_element_type=jnp.float32)
            weighted, denominator = acc[:, :HD], acc[:, HD:]
            if not first:
                shrink = jnp.exp2((tops[0] - m) * (SCALE * LOG2E))
                weighted = weighted + shrink * acc_in[devs, :, lanes].reshape(TILE, HD)
                denominator = denominator + shrink * stat[:, HEADS + h : HEADS + h + 1]
            if last:
                out_ref[devs, :, lanes] = (
                    (weighted / denominator).astype(jnp.bfloat16).reshape(per, ROWS_DEV, HD)
                )
                lse = m * SCALE + jnp.log(denominator)
                high_part = lse.astype(jnp.bfloat16).astype(jnp.float32)
                middle = (lse - high_part).astype(jnp.bfloat16).astype(jnp.float32)
                low_part = lse - high_part - middle
                packed = jnp.where(lane == 3 * h, high_part, packed)
                packed = jnp.where(lane == 3 * h + 1, middle, packed)
                packed = jnp.where(lane == 3 * h + 2, low_part, packed)
            else:
                acc_out[devs, :, lanes] = weighted.reshape(per, ROWS_DEV, HD)
                packed = jnp.where(lane == h, m, packed)
                packed = jnp.where(lane == HEADS + h, denominator, packed)
        if last:
            out_ref[devs, :, HEADS * HD :] = packed.astype(jnp.bfloat16).reshape(
                per, ROWS_DEV, HD
            )
        else:
            stat_out[devs] = packed.reshape(per, ROWS_DEV, HD)
        return carry

    lax.fori_loop(0, PLANE * ROWS_DEV // TILE, row_tile, 0)


def attend(lengths, place, q, blocks, pieces, state, last):
    vmem = pl.BlockSpec(memory_space=pltpu.VMEM)
    smem = pl.BlockSpec(memory_space=pltpu.SMEM)
    keys = sum(high - low for spans in pieces for low, high, masked in spans)
    pairs = PLANE * ROWS_DEV * HEADS * keys
    if last:
        out_shape = jax.ShapeDtypeStruct((PLANE, ROWS_DEV, HEADS * HD + HD), jnp.bfloat16)
        out_specs = vmem
    else:
        out_shape = (
            jax.ShapeDtypeStruct((PLANE, ROWS_DEV, HEADS * HD), jnp.float32),
            jax.ShapeDtypeStruct((PLANE, ROWS_DEV, HD), jnp.float32),
        )
        out_specs = (vmem, vmem)
    return pl.pallas_call(
        functools.partial(attend_kernel, pieces, not state, last),
        in_specs=[smem, smem] + [vmem] * (1 + len(blocks) + len(state)),
        out_specs=out_specs,
        out_shape=out_shape,
        scratch_shapes=[pltpu.VMEM((block.shape[0], 2 * HD), jnp.bfloat16) for block in blocks],
        compiler_params=pltpu.CompilerParams(vmem_limit_bytes=40 * MIB),
        cost_estimate=pl.CostEstimate(
            flops=8 * HD * pairs, bytes_accessed=512 * keys + 2 * MIB, transcendentals=pairs
        ),
        name="attend",
    )(lengths, place, q, *blocks, *state)


def finish_kernel(
    place_ref, q_ref, prompt_ref, acc_ref, stat_ref, out_ref, key_ref, value_ref, sems
):
    chunks = key_ref.shape[0] // CHUNK
    half = -(-chunks // 2)
    copies = []
    for i in range(chunks):
        source = pl.ds(pl.multiple_of(lax.rem(place_ref[3] + 1 + i, chunks + 1) * CHUNK, CHUNK), CHUNK)
        target = pl.ds(i * CHUNK, CHUNK)
        copies.append(
            (
                pltpu.make_async_copy(
                    prompt_ref.at[source, pl.ds(0, HD)], key_ref.at[target, :], sems.at[2 * i]
                ),
                pltpu.make_async_copy(
                    prompt_ref.at[source, pl.ds(HD, HD)],
                    value_ref.at[target, pl.ds(0, HD)],
                    sems.at[2 * i + 1],
                ),
            )
        )
    for key_copy, value_copy in copies:
        key_copy.start()
        value_copy.start()
    value_ref[:, HD:] = jnp.ones((value_ref.shape[0], HD), jnp.bfloat16)
    lane = lax.broadcasted_iota(jnp.int32, (TILE, HD), 1)
    stat = stat_ref[...].reshape(TILE, HD)
    packed = jnp.zeros((TILE, HD), jnp.float32)
    for pair_copies in copies:
        for copy in pair_copies:
            copy.wait()
    for h in range(HEADS):
        lanes = slice(h * HD, (h + 1) * HD)
        q = q_ref[:, :, lanes].reshape(TILE, HD)
        m = stat[:, h : h + 1]
        weighted = acc_ref[:, :, lanes].reshape(TILE, HD)
        denominator = stat[:, HEADS + h : HEADS + h + 1]
        for low, high in ((0, half * CHUNK), (half * CHUNK, chunks * CHUNK)):
            s = nt(q, key_ref[low:high, :])
            raised = jnp.maximum(m, jnp.max(s, axis=1, keepdims=True))
            shrink = jnp.exp2((m - raised) * (SCALE * LOG2E))
            p = jnp.exp2((s - raised) * (SCALE * LOG2E)).astype(jnp.bfloat16)
            acc = jnp.dot(p, value_ref[low:high, :], preferred_element_type=jnp.float32)
            weighted = weighted * shrink + acc[:, :HD]
            denominator = denominator * shrink + acc[:, HD:]
            m = raised
        out_ref[:, :, lanes] = (
            (weighted / denominator).astype(jnp.bfloat16).reshape(PLANE, ROWS_DEV, HD)
        )
        lse = m * SCALE + jnp.log(denominator)
        high_part = lse.astype(jnp.bfloat16).astype(jnp.float32)
        middle = (lse - high_part).astype(jnp.bfloat16).astype(jnp.float32)
        low_part = lse - high_part - middle
        packed = jnp.where(lane == 3 * h, high_part, packed)
        packed = jnp.where(lane == 3 * h + 1, middle, packed)
        packed = jnp.where(lane == 3 * h + 2, low_part, packed)
    out_ref[:, :, HEADS * HD :] = packed.astype(jnp.bfloat16).reshape(PLANE, ROWS_DEV, HD)


def finish(place, q, prompt, state):
    vmem = pl.BlockSpec(memory_space=pltpu.VMEM)
    smem = pl.BlockSpec(memory_space=pltpu.SMEM)
    keys = prompt.shape[0] - CHUNK
    pairs = PLANE * ROWS_DEV * HEADS * keys
    return pl.pallas_call(
        finish_kernel,
        in_specs=[smem, vmem, pl.BlockSpec(memory_space=pltpu.HBM), vmem, vmem],
        out_specs=vmem,
        out_shape=jax.ShapeDtypeStruct((PLANE, ROWS_DEV, HEADS * HD + HD), jnp.bfloat16),
        scratch_shapes=[
            pltpu.VMEM((keys, HD), jnp.bfloat16),
            pltpu.VMEM((keys, 2 * HD), jnp.bfloat16),
            pltpu.SemaphoreType.DMA((2 * (keys // CHUNK),)),
        ],
        compiler_params=pltpu.CompilerParams(vmem_limit_bytes=61 * MIB),
        cost_estimate=pl.CostEstimate(
            flops=8 * HD * pairs, bytes_accessed=512 * keys + 2 * MIB, transcendentals=pairs
        ),
        name="finish",
    )(place, q, prompt, *state)


def combine_kernel(parts_ref, out_ref):
    tops = []
    for j in range(PLANE):
        bits = parts_ref[j, :, HEADS * HD :].astype(jnp.float32)
        tops.append(bits + pltpu.roll(bits, HD - 1, 1) + pltpu.roll(bits, HD - 2, 1))
    top = jnp.maximum(jnp.maximum(tops[0], tops[1]), jnp.maximum(tops[2], tops[3]))
    weights = [jnp.exp(x - top) for x in tops]
    share = 1.0 / (weights[0] + weights[1] + weights[2] + weights[3])
    weights = [x * share for x in weights]
    heads = []
    for h in range(HEADS):
        lanes = slice(h * HD, (h + 1) * HD)
        heads.append(
            sum(
                weights[j][:, 3 * h : 3 * h + 1] * parts_ref[j, :, lanes].astype(jnp.float32)
                for j in range(PLANE)
            )
        )
    out_ref[...] = jnp.stack(heads, axis=1).astype(jnp.bfloat16)


def combine(parts):
    rows = 64
    return pl.pallas_call(
        combine_kernel,
        grid=(ROWS_DEV // rows,),
        in_specs=[pl.BlockSpec((PLANE, rows, HEADS * HD + HD), lambda i: (0, i, 0))],
        out_specs=pl.BlockSpec((rows, HEADS, HD), lambda i: (i, 0, 0)),
        out_shape=jax.ShapeDtypeStruct((ROWS_DEV, HEADS, HD), jnp.bfloat16),
        name="combine",
    )(parts)


def to_all(x, axes, count):
    return lax.all_to_all(jnp.broadcast_to(x[None], (count,) + x.shape), axes, 0, 0)


def shards(queries, prompt_kv, response_kv, logits, token_ids, lengths, rewards):
    pair = lax.axis_index("zh")
    z = lax.axis_index(Z)
    row = lax.axis_index("yl")
    core = lax.axis_index("core")
    pairs = lax.axis_size("zh")
    responses = lengths.shape[0]
    pb = prompt_kv.shape[0]
    rb = response_kv.shape[0]

    own_prompt = prompt_kv.reshape(pb, 2 * HD)
    prompt = lax.all_gather(own_prompt, ("zh", "core"), axis=0, tiled=True)
    q = to_all(queries.reshape(ROWS_DEV, HEADS * HD), SHARE, PLANE)

    vocab_base = (lax.axis_index("tp") * logits.shape[1]).astype(jnp.int32).reshape(1)
    stats = logit_stats(logits, token_ids, vocab_base, lax.axis_size("tp"))
    stats = lax.all_to_all(stats, "tp", 0, 0)

    own = response_kv.reshape(rb, 2 * HD)
    before = [
        lax.ppermute(own, "zh", [(i, (i + d) % pairs) for i in range(pairs)]) for d in (1, 2)
    ]
    mine = jnp.concatenate([own_prompt, own] + before, axis=0)
    other = lax.ppermute(mine, "core", [(0, 1), (1, 0)])

    peaks, sums, picks = stats[:, 0], stats[:, 1], stats[:, 2]
    peak = jnp.max(peaks, axis=0)
    spread = jnp.sum(sums * jnp.exp(peaks - peak), axis=0)
    logprob = jnp.sum(picks, axis=0) - peak - jnp.log(spread)
    ends_at = jnp.cumsum(lengths)
    block = z * PLANE + row * 2
    rows = (block + core) * ROWS_DEV + jnp.arange(ROWS_DEV, dtype=jnp.int32)
    segment = jnp.sum((rows[:, None] >= ends_at[None, :]).astype(jnp.int32), axis=1)
    token_logprob = jnp.where(segment < responses, logprob, 0.0)
    members = segment[:, None] == jnp.arange(128, dtype=jnp.int32)[None, :]
    part = jnp.sum(jnp.where(members, token_logprob[:, None], 0.0), axis=0)
    part = jnp.sum(to_all(part[None], CTX, 64)[:, 0], axis=0)
    response_sum = part[:responses]
    length_float = lengths.astype(jnp.float32)
    adjusted = rewards - 0.5 * length_float / 2048
    advantage = adjusted - jnp.mean(adjusted)
    response_objective = -advantage * response_sum / length_float

    first_row = (pair * 2 * PLANE + core) * ROWS_DEV
    place = jnp.stack(
        [first_row, (block + core) * ROWS_DEV, (block + 1 - core) * ROWS_DEV, pair]
    ).astype(jnp.int32)
    spans = ((0, pb, False), (pb, pb + 3 * rb, True))
    state = attend(lengths, place, q, [mine, other], [spans, spans], (), False)
    partial = finish(place, q, prompt, state)
    exchanged = lax.all_to_all(partial, SHARE, 0, 0)
    context = combine(exchanged)
    return (context, token_logprob, response_objective)


def solution(mesh):
    fine = Mesh(mesh.devices.reshape(8, 2, 2, 2, 8), ("zh", "zl", "yl", "core", "tp"))
    return jax.shard_map(
        shards,
        mesh=fine,
        in_specs=(
            P(CTX, "tp", None),
            P(CTX, None, "tp", None),
            P(CTX, None, "tp", None),
            P(CTX, "tp"),
            P(CTX),
            P(),
            P(),
        ),
        out_specs=(P(CTX, "tp", None), P(CTX), P()),
        check_vma=False,
    )
```

```python
import functools
import math

import jax
import jax.numpy as jnp
from jax import lax
from jax.experimental import pallas as pl
from jax.experimental.pallas import tpu as pltpu
from jax.sharding import Mesh, PartitionSpec as P

HD = 128
HEADS = 4
ROWS_DEV = 128
PLANE = 4
TILE = 512
SCALE = 1.0 / math.sqrt(HD)
LOG2E = 1.4426950408889634
Z = ("zh", "zl")
CTX = Z + ("yl", "core")
SHARE = ("zl", "yl")
MIB = 1 << 20


def logit_kernel(token_ref, base_ref, logits_ref, out_ref, stat_ref, target_ref):
    step = pl.program_id(0)
    rows, width = logits_ref.shape

    @pl.when(step == 0)
    def _():
        wanted = jnp.broadcast_to(token_ref[...].astype(jnp.float32), target_ref.shape)
        target_ref[...] = wanted.T.astype(jnp.int32) - base_ref[0]

    here = pl.ds(pl.multiple_of(step * rows, rows), rows)
    wide = logits_ref[...].astype(jnp.float32)
    peak = jnp.max(wide, axis=1, keepdims=True)
    total = jnp.sum(jnp.exp(wide - peak), axis=1, keepdims=True)
    columns = lax.broadcasted_iota(jnp.int32, (rows, width), 1)
    matches = columns == target_ref[here, :1]
    picked = jnp.sum(jnp.where(matches, wide, 0.0), axis=1, keepdims=True)
    lane = lax.broadcasted_iota(jnp.int32, (rows, 128), 1)
    stat_ref[here, :] = jnp.where(
        lane == 0, peak, jnp.where(lane == 1, total, picked)
    )

    @pl.when(step == pl.num_programs(0) - 1)
    def _():
        out_ref[...] = jnp.broadcast_to(stat_ref[...].T[None, :8], out_ref.shape)


def logit_stats(logits, token_ids, vocab_base, copies):
    rows, width = logits.shape
    block = 32
    return pl.pallas_call(
        logit_kernel,
        grid=(rows // block,),
        in_specs=[
            pl.BlockSpec((1, rows), lambda i: (0, 0)),
            pl.BlockSpec(memory_space=pltpu.SMEM),
            pl.BlockSpec((block, width), lambda i: (i, 0)),
        ],
        out_specs=pl.BlockSpec((copies, 8, rows), lambda i: (0, 0, 0)),
        out_shape=jax.ShapeDtypeStruct((copies, 8, rows), jnp.float32),
        scratch_shapes=[pltpu.VMEM((rows, 128), jnp.float32), pltpu.VMEM((rows, 128), jnp.int32)],
        compiler_params=pltpu.CompilerParams(vmem_limit_bytes=32 * MIB),
        cost_estimate=pl.CostEstimate(
            flops=8 * rows * width, bytes_accessed=2 * rows * width, transcendentals=rows * width
        ),
        name="logit_stats",
    )(token_ids.reshape(1, rows), vocab_base, logits)


def nt(a, b):
    return lax.dot_general(a, b, (((1,), (1,)), ((), ())), preferred_element_type=jnp.float32)


def attend_kernel(pieces, first, last, *refs):
    lengths_ref, place_ref, q_ref = refs[:3]
    count = len(pieces)
    kv_refs = refs[3 : 3 + count]
    refs = refs[3 + count :]
    if not first:
        acc_in, stat_in = refs[:2]
        refs = refs[2:]
    if last:
        out_ref = refs[0]
        refs = refs[1:]
    else:
        acc_out, stat_out = refs[:2]
        refs = refs[2:]
    v_refs = refs
    for kv_ref, v_ref in zip(kv_refs, v_refs):
        v_ref[:, :HD] = kv_ref[:, HD:]
        v_ref[:, HD:] = jnp.ones((kv_ref.shape[0], HD), jnp.bfloat16)
    lane = lax.broadcasted_iota(jnp.int32, (TILE, HD), 1)
    per = TILE // ROWS_DEV

    def row_tile(t, carry):
        index = t * TILE + lax.broadcasted_iota(jnp.int32, (TILE, 1), 0)
        planes, spots = index // (2 * ROWS_DEV), index // ROWS_DEV % 2
        rows = place_ref[0] + (planes * PLANE + spots * 2) * ROWS_DEV + index % ROWS_DEV
        start = jnp.zeros((TILE, 1), jnp.int32)
        edge = jnp.int32(0)
        for r in range(lengths_ref.shape[0]):
            edge = edge + lengths_ref[r]
            start = jnp.where(rows >= edge, edge, start)
        start = jnp.where(rows >= edge, rows, start)
        devs = pl.ds(t * per, per)
        packed = jnp.zeros((TILE, HD), jnp.float32)
        if not first:
            stat = stat_in[devs].reshape(TILE, HD)
        for h in range(HEADS):
            lanes = slice(h * HD, (h + 1) * HD)
            q = q_ref[devs, :, lanes].reshape(TILE, HD)
            if first:
                m = jnp.full((TILE, 1), -1e30, jnp.float32)
                weighted = jnp.zeros((TILE, HD), jnp.float32)
                denominator = jnp.zeros((TILE, HD), jnp.float32)
            else:
                m = stat[:, h : h + 1]
                weighted = acc_in[devs, :, lanes].reshape(TILE, HD)
                denominator = stat[:, HEADS + h : HEADS + h + 1]
            answer = 0
            for kv_ref, v_ref, spans in zip(kv_refs, v_refs, pieces):
                for low, high, masked in spans:
                    s = nt(q, kv_ref[low:high, :HD])
                    if masked:
                        answer += 1
                        column = lax.broadcasted_iota(jnp.int32, (TILE, high - low), 1)
                        keys = place_ref[answer] + column % ROWS_DEV
                        keys = keys - column // ROWS_DEV * (2 * PLANE * ROWS_DEV)
                        s = jnp.where((keys >= start) & (keys <= rows), s, -1e30)
                    raised = jnp.maximum(m, jnp.max(s, axis=1, keepdims=True))
                    shrink = jnp.exp2((m - raised) * (SCALE * LOG2E))
                    p = jnp.exp2((s - raised) * (SCALE * LOG2E)).astype(jnp.bfloat16)
                    acc = jnp.dot(p, v_ref[low:high, :], preferred_element_type=jnp.float32)
                    weighted = weighted * shrink + acc[:, :HD]
                    denominator = denominator * shrink + acc[:, HD:]
                    m = raised
            if last:
                out_ref[devs, :, lanes] = (
                    (weighted / denominator).astype(jnp.bfloat16).reshape(per, ROWS_DEV, HD)
                )
                lse = m * SCALE + jnp.log(denominator)
                high_part = lse.astype(jnp.bfloat16).astype(jnp.float32)
                middle = (lse - high_part).astype(jnp.bfloat16).astype(jnp.float32)
                low_part = lse - high_part - middle
                packed = jnp.where(lane == 3 * h, high_part, packed)
                packed = jnp.where(lane == 3 * h + 1, middle, packed)
                packed = jnp.where(lane == 3 * h + 2, low_part, packed)
            else:
                acc_out[devs, :, lanes] = weighted.reshape(per, ROWS_DEV, HD)
                packed = jnp.where(lane == h, m, packed)
                packed = jnp.where(lane == HEADS + h, denominator, packed)
        if last:
            out_ref[devs, :, HEADS * HD :] = packed.astype(jnp.bfloat16).reshape(
                per, ROWS_DEV, HD
            )
        else:
            stat_out[devs] = packed.reshape(per, ROWS_DEV, HD)
        return carry

    lax.fori_loop(0, PLANE * ROWS_DEV // TILE, row_tile, 0)


def attend(lengths, place, q, blocks, pieces, state, last):
    vmem = pl.BlockSpec(memory_space=pltpu.VMEM)
    smem = pl.BlockSpec(memory_space=pltpu.SMEM)
    keys = sum(high - low for spans in pieces for low, high, masked in spans)
    pairs = PLANE * ROWS_DEV * HEADS * keys
    if last:
        out_shape = jax.ShapeDtypeStruct((PLANE, ROWS_DEV, HEADS * HD + HD), jnp.bfloat16)
        out_specs = vmem
    else:
        out_shape = (
            jax.ShapeDtypeStruct((PLANE, ROWS_DEV, HEADS * HD), jnp.float32),
            jax.ShapeDtypeStruct((PLANE, ROWS_DEV, HD), jnp.float32),
        )
        out_specs = (vmem, vmem)
    return pl.pallas_call(
        functools.partial(attend_kernel, pieces, not state, last),
        in_specs=[smem, smem] + [vmem] * (1 + len(blocks) + len(state)),
        out_specs=out_specs,
        out_shape=out_shape,
        scratch_shapes=[pltpu.VMEM((block.shape[0], 2 * HD), jnp.bfloat16) for block in blocks],
        compiler_params=pltpu.CompilerParams(vmem_limit_bytes=40 * MIB),
        cost_estimate=pl.CostEstimate(
            flops=8 * HD * pairs, bytes_accessed=512 * keys + 2 * MIB, transcendentals=pairs
        ),
        name="attend",
    )(lengths, place, q, *blocks, *state)


def combine_kernel(parts_ref, out_ref):
    tops = []
    for j in range(PLANE):
        bits = parts_ref[j, :, HEADS * HD :].astype(jnp.float32)
        tops.append(bits + pltpu.roll(bits, HD - 1, 1) + pltpu.roll(bits, HD - 2, 1))
    top = jnp.maximum(jnp.maximum(tops[0], tops[1]), jnp.maximum(tops[2], tops[3]))
    weights = [jnp.exp(x - top) for x in tops]
    share = 1.0 / (weights[0] + weights[1] + weights[2] + weights[3])
    weights = [x * share for x in weights]
    heads = []
    for h in range(HEADS):
        lanes = slice(h * HD, (h + 1) * HD)
        heads.append(
            sum(
                weights[j][:, 3 * h : 3 * h + 1] * parts_ref[j, :, lanes].astype(jnp.float32)
                for j in range(PLANE)
            )
        )
    out_ref[...] = jnp.stack(heads, axis=1).astype(jnp.bfloat16)


def combine(parts):
    rows = 64
    return pl.pallas_call(
        combine_kernel,
        grid=(ROWS_DEV // rows,),
        in_specs=[pl.BlockSpec((PLANE, rows, HEADS * HD + HD), lambda i: (0, i, 0))],
        out_specs=pl.BlockSpec((rows, HEADS, HD), lambda i: (i, 0, 0)),
        out_shape=jax.ShapeDtypeStruct((ROWS_DEV, HEADS, HD), jnp.bfloat16),
        name="combine",
    )(parts)


def to_all(x, axes, count):
    return lax.all_to_all(jnp.broadcast_to(x[None], (count,) + x.shape), axes, 0, 0)


def shards(queries, prompt_kv, response_kv, logits, token_ids, lengths, rewards):
    pair = lax.axis_index("zh")
    z = lax.axis_index(Z)
    row = lax.axis_index("yl")
    core = lax.axis_index("core")
    pairs = lax.axis_size("zh")
    responses = lengths.shape[0]
    pb = prompt_kv.shape[0]
    rb = response_kv.shape[0]

    prompt = lax.all_gather(prompt_kv.reshape(pb, 2 * HD), ("zh", "core"), axis=0, tiled=True)
    q = to_all(queries.reshape(ROWS_DEV, HEADS * HD), SHARE, PLANE)

    vocab_base = (lax.axis_index("tp") * logits.shape[1]).astype(jnp.int32).reshape(1)
    stats = logit_stats(logits, token_ids, vocab_base, lax.axis_size("tp"))
    stats, q = lax.optimization_barrier((stats, q))
    stats = lax.all_to_all(stats, "tp", 0, 0)

    own = response_kv.reshape(rb, 2 * HD)
    before = [
        lax.ppermute(own, "zh", [(i, (i + d) % pairs) for i in range(pairs)]) for d in (1, 2)
    ]
    mine = jnp.concatenate([own] + before, axis=0)
    other = lax.ppermute(mine, "core", [(0, 1), (1, 0)])

    peaks, sums, picks = stats[:, 0], stats[:, 1], stats[:, 2]
    peak = jnp.max(peaks, axis=0)
    spread = jnp.sum(sums * jnp.exp(peaks - peak), axis=0)
    logprob = jnp.sum(picks, axis=0) - peak - jnp.log(spread)
    ends_at = jnp.cumsum(lengths)
    block = z * PLANE + row * 2
    rows = (block + core) * ROWS_DEV + jnp.arange(ROWS_DEV, dtype=jnp.int32)
    segment = jnp.sum((rows[:, None] >= ends_at[None, :]).astype(jnp.int32), axis=1)
    token_logprob = jnp.where(segment < responses, logprob, 0.0)
    members = segment[:, None] == jnp.arange(128, dtype=jnp.int32)[None, :]
    part = jnp.sum(jnp.where(members, token_logprob[:, None], 0.0), axis=0)
    part = jnp.sum(to_all(part[None], ("zl", "yl", "core"), 8)[:, 0], axis=0)

    first_row = (pair * 2 * PLANE + core) * ROWS_DEV
    place = jnp.stack(
        [first_row, (block + core) * ROWS_DEV, (block + 1 - core) * ROWS_DEV]
    ).astype(jnp.int32)
    masked = ((0, 3 * rb, True),)
    state = attend(lengths, place, q, [mine, other], [masked, masked], (), False)
    half = prompt.shape[0] // 2
    part, _ = lax.optimization_barrier((part, state[1]))
    part = jnp.sum(to_all(part[None], "zh", pairs)[:, 0], axis=0)
    spans = ((0, half, False), (half, 2 * half, False))
    partial = attend(lengths, place, q, [prompt], [spans], state, True)
    exchanged = lax.all_to_all(partial, SHARE, 0, 0)
    context = combine(exchanged)

    response_sum = part[:responses]
    length_float = lengths.astype(jnp.float32)
    adjusted = rewards - 0.5 * length_float / 2048
    advantage = adjusted - jnp.mean(adjusted)
    response_objective = -advantage * response_sum / length_float
    return (context, token_logprob, response_objective)


def solution(mesh):
    fine = Mesh(mesh.devices.reshape(8, 2, 2, 2, 8), ("zh", "zl", "yl", "core", "tp"))
    return jax.shard_map(
        shards,
        mesh=fine,
        in_specs=(
            P(CTX, "tp", None),
            P(CTX, None, "tp", None),
            P(CTX, None, "tp", None),
            P(CTX, "tp"),
            P(CTX),
            P(),
            P(),
        ),
        out_specs=(P(CTX, "tp", None), P(CTX), P()),
        check_vma=False,
    )
```

```python
import functools
import math

import jax
import jax.numpy as jnp
from jax import lax
from jax.experimental import pallas as pl
from jax.experimental.pallas import tpu as pltpu
from jax.sharding import Mesh, PartitionSpec as P

HD = 128
HEADS = 4
ROWS_DEV = 128
PLANE = 4
TILE = 512
SCALE = 1.0 / math.sqrt(HD)
LOG2E = 1.4426950408889634
Z = ("zh", "zl")
CTX = Z + ("yl", "core")
SHARE = ("zl", "yl")
MIB = 1 << 20


def logit_kernel(token_ref, base_ref, logits_ref, out_ref, stat_ref, target_ref):
    step = pl.program_id(0)
    rows, width = logits_ref.shape

    @pl.when(step == 0)
    def _():
        wanted = jnp.broadcast_to(token_ref[...].astype(jnp.float32), target_ref.shape)
        target_ref[...] = wanted.T.astype(jnp.int32) - base_ref[0]

    here = pl.ds(pl.multiple_of(step * rows, rows), rows)
    wide = logits_ref[...].astype(jnp.float32)
    peak = jnp.max(wide, axis=1, keepdims=True)
    total = jnp.sum(jnp.exp(wide - peak), axis=1, keepdims=True)
    columns = lax.broadcasted_iota(jnp.int32, (rows, width), 1)
    matches = columns == target_ref[here, :1]
    picked = jnp.sum(jnp.where(matches, wide, 0.0), axis=1, keepdims=True)
    lane = lax.broadcasted_iota(jnp.int32, (rows, 128), 1)
    stat_ref[here, :] = jnp.where(
        lane == 0, peak, jnp.where(lane == 1, total, picked)
    )

    @pl.when(step == pl.num_programs(0) - 1)
    def _():
        out_ref[...] = jnp.broadcast_to(stat_ref[...].T[None, :8], out_ref.shape)


def logit_stats(logits, token_ids, vocab_base, copies):
    rows, width = logits.shape
    block = 32
    return pl.pallas_call(
        logit_kernel,
        grid=(rows // block,),
        in_specs=[
            pl.BlockSpec((1, rows), lambda i: (0, 0)),
            pl.BlockSpec(memory_space=pltpu.SMEM),
            pl.BlockSpec((block, width), lambda i: (i, 0)),
        ],
        out_specs=pl.BlockSpec((copies, 8, rows), lambda i: (0, 0, 0)),
        out_shape=jax.ShapeDtypeStruct((copies, 8, rows), jnp.float32),
        scratch_shapes=[pltpu.VMEM((rows, 128), jnp.float32), pltpu.VMEM((rows, 128), jnp.int32)],
        compiler_params=pltpu.CompilerParams(vmem_limit_bytes=32 * MIB),
        cost_estimate=pl.CostEstimate(
            flops=8 * rows * width, bytes_accessed=2 * rows * width, transcendentals=rows * width
        ),
        name="logit_stats",
    )(token_ids.reshape(1, rows), vocab_base, logits)


def nt(a, b):
    return lax.dot_general(a, b, (((1,), (1,)), ((), ())), preferred_element_type=jnp.float32)


def attend_kernel(pieces, first, last, *refs):
    lengths_ref, place_ref, q_ref = refs[:3]
    count = len(pieces)
    kv_refs = refs[3 : 3 + count]
    refs = refs[3 + count :]
    if not first:
        acc_in, stat_in = refs[:2]
        refs = refs[2:]
    if last:
        out_ref = refs[0]
        refs = refs[1:]
    else:
        acc_out, stat_out = refs[:2]
        refs = refs[2:]
    v_refs = refs
    for kv_ref, v_ref in zip(kv_refs, v_refs):
        v_ref[:, :HD] = kv_ref[:, HD:]
        v_ref[:, HD:] = jnp.ones((kv_ref.shape[0], HD), jnp.bfloat16)
    lane = lax.broadcasted_iota(jnp.int32, (TILE, HD), 1)
    per = TILE // ROWS_DEV

    def row_tile(t, carry):
        index = t * TILE + lax.broadcasted_iota(jnp.int32, (TILE, 1), 0)
        planes, spots = index // (2 * ROWS_DEV), index // ROWS_DEV % 2
        rows = place_ref[0] + (planes * PLANE + spots * 2) * ROWS_DEV + index % ROWS_DEV
        start = jnp.zeros((TILE, 1), jnp.int32)
        edge = jnp.int32(0)
        for r in range(lengths_ref.shape[0]):
            edge = edge + lengths_ref[r]
            start = jnp.where(rows >= edge, edge, start)
        start = jnp.where(rows >= edge, rows, start)
        devs = pl.ds(t * per, per)
        packed = jnp.zeros((TILE, HD), jnp.float32)
        if not first:
            stat = stat_in[devs].reshape(TILE, HD)
        for h in range(HEADS):
            lanes = slice(h * HD, (h + 1) * HD)
            q = q_ref[devs, :, lanes].reshape(TILE, HD)
            if first:
                m = jnp.full((TILE, 1), -1e30, jnp.float32)
                weighted = jnp.zeros((TILE, HD), jnp.float32)
                denominator = jnp.zeros((TILE, HD), jnp.float32)
            else:
                m = stat[:, h : h + 1]
                weighted = acc_in[devs, :, lanes].reshape(TILE, HD)
                denominator = stat[:, HEADS + h : HEADS + h + 1]
            answer = 0
            for kv_ref, v_ref, spans in zip(kv_refs, v_refs, pieces):
                for low, high, masked in spans:
                    s = nt(q, kv_ref[low:high, :HD])
                    if masked:
                        answer += 1
                        column = lax.broadcasted_iota(jnp.int32, (TILE, high - low), 1)
                        keys = place_ref[answer] + column % ROWS_DEV
                        keys = keys - column // ROWS_DEV * (2 * PLANE * ROWS_DEV)
                        s = jnp.where((keys >= start) & (keys <= rows), s, -1e30)
                    raised = jnp.maximum(m, jnp.max(s, axis=1, keepdims=True))
                    shrink = jnp.exp2((m - raised) * (SCALE * LOG2E))
                    p = jnp.exp2((s - raised) * (SCALE * LOG2E)).astype(jnp.bfloat16)
                    acc = jnp.dot(p, v_ref[low:high, :], preferred_element_type=jnp.float32)
                    weighted = weighted * shrink + acc[:, :HD]
                    denominator = denominator * shrink + acc[:, HD:]
                    m = raised
            if last:
                out_ref[devs, :, lanes] = (
                    (weighted / denominator).astype(jnp.bfloat16).reshape(per, ROWS_DEV, HD)
                )
                lse = m * SCALE + jnp.log(denominator)
                high_part = lse.astype(jnp.bfloat16).astype(jnp.float32)
                middle = (lse - high_part).astype(jnp.bfloat16).astype(jnp.float32)
                low_part = lse - high_part - middle
                packed = jnp.where(lane == 3 * h, high_part, packed)
                packed = jnp.where(lane == 3 * h + 1, middle, packed)
                packed = jnp.where(lane == 3 * h + 2, low_part, packed)
            else:
                acc_out[devs, :, lanes] = weighted.reshape(per, ROWS_DEV, HD)
                packed = jnp.where(lane == h, m, packed)
                packed = jnp.where(lane == HEADS + h, denominator, packed)
        if last:
            out_ref[devs, :, HEADS * HD :] = packed.astype(jnp.bfloat16).reshape(
                per, ROWS_DEV, HD
            )
        else:
            stat_out[devs] = packed.reshape(per, ROWS_DEV, HD)
        return carry

    lax.fori_loop(0, PLANE * ROWS_DEV // TILE, row_tile, 0)


def attend(lengths, place, q, blocks, pieces, state, last):
    vmem = pl.BlockSpec(memory_space=pltpu.VMEM)
    smem = pl.BlockSpec(memory_space=pltpu.SMEM)
    keys = sum(high - low for spans in pieces for low, high, masked in spans)
    pairs = PLANE * ROWS_DEV * HEADS * keys
    if last:
        out_shape = jax.ShapeDtypeStruct((PLANE, ROWS_DEV, HEADS * HD + HD), jnp.bfloat16)
        out_specs = vmem
    else:
        out_shape = (
            jax.ShapeDtypeStruct((PLANE, ROWS_DEV, HEADS * HD), jnp.float32),
            jax.ShapeDtypeStruct((PLANE, ROWS_DEV, HD), jnp.float32),
        )
        out_specs = (vmem, vmem)
    return pl.pallas_call(
        functools.partial(attend_kernel, pieces, not state, last),
        in_specs=[smem, smem] + [vmem] * (1 + len(blocks) + len(state)),
        out_specs=out_specs,
        out_shape=out_shape,
        scratch_shapes=[pltpu.VMEM((block.shape[0], 2 * HD), jnp.bfloat16) for block in blocks],
        compiler_params=pltpu.CompilerParams(vmem_limit_bytes=40 * MIB),
        cost_estimate=pl.CostEstimate(
            flops=8 * HD * pairs, bytes_accessed=512 * keys + 2 * MIB, transcendentals=pairs
        ),
        name="attend",
    )(lengths, place, q, *blocks, *state)


def combine_kernel(parts_ref, out_ref):
    tops = []
    for j in range(PLANE):
        bits = parts_ref[j, :, HEADS * HD :].astype(jnp.float32)
        tops.append(bits + pltpu.roll(bits, HD - 1, 1) + pltpu.roll(bits, HD - 2, 1))
    top = jnp.maximum(jnp.maximum(tops[0], tops[1]), jnp.maximum(tops[2], tops[3]))
    weights = [jnp.exp(x - top) for x in tops]
    share = 1.0 / (weights[0] + weights[1] + weights[2] + weights[3])
    weights = [x * share for x in weights]
    heads = []
    for h in range(HEADS):
        lanes = slice(h * HD, (h + 1) * HD)
        heads.append(
            sum(
                weights[j][:, 3 * h : 3 * h + 1] * parts_ref[j, :, lanes].astype(jnp.float32)
                for j in range(PLANE)
            )
        )
    out_ref[...] = jnp.stack(heads, axis=1).astype(jnp.bfloat16)


def combine(parts):
    rows = 64
    return pl.pallas_call(
        combine_kernel,
        grid=(ROWS_DEV // rows,),
        in_specs=[pl.BlockSpec((PLANE, rows, HEADS * HD + HD), lambda i: (0, i, 0))],
        out_specs=pl.BlockSpec((rows, HEADS, HD), lambda i: (i, 0, 0)),
        out_shape=jax.ShapeDtypeStruct((ROWS_DEV, HEADS, HD), jnp.bfloat16),
        name="combine",
    )(parts)


def to_all(x, axes, count):
    return lax.all_to_all(jnp.broadcast_to(x[None], (count,) + x.shape), axes, 0, 0)


def shards(queries, prompt_kv, response_kv, logits, token_ids, lengths, rewards):
    pair = lax.axis_index("zh")
    z = lax.axis_index(Z)
    row = lax.axis_index("yl")
    core = lax.axis_index("core")
    pairs = lax.axis_size("zh")
    responses = lengths.shape[0]
    pb = prompt_kv.shape[0]
    rb = response_kv.shape[0]

    prompt = lax.all_gather(prompt_kv.reshape(pb, 2 * HD), ("zh", "core"), axis=0, tiled=True)
    q = to_all(queries.reshape(ROWS_DEV, HEADS * HD), SHARE, PLANE)

    vocab_base = (lax.axis_index("tp") * logits.shape[1]).astype(jnp.int32).reshape(1)
    stats = logit_stats(logits, token_ids, vocab_base, lax.axis_size("tp"))
    stats, q = lax.optimization_barrier((stats, q))
    stats = lax.all_to_all(stats, "tp", 0, 0)

    own = response_kv.reshape(rb, 2 * HD)
    route = [(i, (i + 1) % pairs) for i in range(pairs)]
    once = lax.ppermute(own, "zh", route)
    before = [once, lax.ppermute(once, "zh", route)]
    mine = jnp.concatenate([own] + before, axis=0)
    other = lax.ppermute(mine, "core", [(0, 1), (1, 0)])

    peaks, sums, picks = stats[:, 0], stats[:, 1], stats[:, 2]
    peak = jnp.max(peaks, axis=0)
    spread = jnp.sum(sums * jnp.exp(peaks - peak), axis=0)
    logprob = jnp.sum(picks, axis=0) - peak - jnp.log(spread)
    ends_at = jnp.cumsum(lengths)
    block = z * PLANE + row * 2
    rows = (block + core) * ROWS_DEV + jnp.arange(ROWS_DEV, dtype=jnp.int32)
    segment = jnp.sum((rows[:, None] >= ends_at[None, :]).astype(jnp.int32), axis=1)
    token_logprob = jnp.where(segment < responses, logprob, 0.0)
    members = segment[:, None] == jnp.arange(128, dtype=jnp.int32)[None, :]
    part = jnp.sum(jnp.where(members, token_logprob[:, None], 0.0), axis=0)
    part = jnp.sum(to_all(part[None], ("zl", "yl", "core"), 8)[:, 0], axis=0)

    first_row = (pair * 2 * PLANE + core) * ROWS_DEV
    place = jnp.stack(
        [first_row, (block + core) * ROWS_DEV, (block + 1 - core) * ROWS_DEV]
    ).astype(jnp.int32)
    masked = ((0, 3 * rb, True),)
    state = attend(lengths, place, q, [mine, other], [masked, masked], (), False)
    half = prompt.shape[0] // 2
    part, _ = lax.optimization_barrier((part, state[1]))
    part = jnp.sum(to_all(part[None], "zh", pairs)[:, 0], axis=0)
    spans = ((0, half, False), (half, 2 * half, False))
    partial = attend(lengths, place, q, [prompt], [spans], state, True)
    exchanged = lax.all_to_all(partial, SHARE, 0, 0)
    context = combine(exchanged)

    response_sum = part[:responses]
    length_float = lengths.astype(jnp.float32)
    adjusted = rewards - 0.5 * length_float / 2048
    advantage = adjusted - jnp.mean(adjusted)
    response_objective = -advantage * response_sum / length_float
    return (context, token_logprob, response_objective)


def solution(mesh):
    fine = Mesh(mesh.devices.reshape(8, 2, 2, 2, 8), ("zh", "zl", "yl", "core", "tp"))
    return jax.shard_map(
        shards,
        mesh=fine,
        in_specs=(
            P(CTX, "tp", None),
            P(CTX, None, "tp", None),
            P(CTX, None, "tp", None),
            P(CTX, "tp"),
            P(CTX),
            P(),
            P(),
        ),
        out_specs=(P(CTX, "tp", None), P(CTX), P()),
        check_vma=False,
    )
```

```python
import functools
import math

import jax
import jax.numpy as jnp
from jax import lax
from jax.experimental import pallas as pl
from jax.experimental.pallas import tpu as pltpu
from jax.sharding import Mesh, PartitionSpec as P

HD = 128
HEADS = 4
ROWS_DEV = 128
PLANE = 4
TILE = 512
SCALE = 1.0 / math.sqrt(HD)
LOG2E = 1.4426950408889634
Z = ("zh", "zl")
CTX = Z + ("yl", "core")
SHARE = ("zl", "yl")
MIB = 1 << 20


def logit_kernel(token_ref, base_ref, logits_ref, out_ref, stat_ref, target_ref):
    step = pl.program_id(0)
    rows, width = logits_ref.shape

    @pl.when(step == 0)
    def _():
        wanted = jnp.broadcast_to(token_ref[...].astype(jnp.float32), target_ref.shape)
        target_ref[...] = wanted.T.astype(jnp.int32) - base_ref[0]

    here = pl.ds(pl.multiple_of(step * rows, rows), rows)
    wide = logits_ref[...].astype(jnp.float32)
    peak = jnp.max(wide, axis=1, keepdims=True)
    total = jnp.sum(jnp.exp(wide - peak), axis=1, keepdims=True)
    columns = lax.broadcasted_iota(jnp.int32, (rows, width), 1)
    matches = columns == target_ref[here, :1]
    picked = jnp.sum(jnp.where(matches, wide, 0.0), axis=1, keepdims=True)
    lane = lax.broadcasted_iota(jnp.int32, (rows, 128), 1)
    stat_ref[here, :] = jnp.where(
        lane == 0, peak, jnp.where(lane == 1, total, picked)
    )

    @pl.when(step == pl.num_programs(0) - 1)
    def _():
        out_ref[...] = jnp.broadcast_to(stat_ref[...].T[None, :8], out_ref.shape)


def logit_stats(logits, token_ids, vocab_base, copies):
    rows, width = logits.shape
    block = 32
    return pl.pallas_call(
        logit_kernel,
        grid=(rows // block,),
        in_specs=[
            pl.BlockSpec((1, rows), lambda i: (0, 0)),
            pl.BlockSpec(memory_space=pltpu.SMEM),
            pl.BlockSpec((block, width), lambda i: (i, 0)),
        ],
        out_specs=pl.BlockSpec((copies, 8, rows), lambda i: (0, 0, 0)),
        out_shape=jax.ShapeDtypeStruct((copies, 8, rows), jnp.float32),
        scratch_shapes=[pltpu.VMEM((rows, 128), jnp.float32), pltpu.VMEM((rows, 128), jnp.int32)],
        compiler_params=pltpu.CompilerParams(vmem_limit_bytes=32 * MIB),
        cost_estimate=pl.CostEstimate(
            flops=8 * rows * width, bytes_accessed=2 * rows * width, transcendentals=rows * width
        ),
        name="logit_stats",
    )(token_ids.reshape(1, rows), vocab_base, logits)


def nt(a, b):
    return lax.dot_general(a, b, (((1,), (1,)), ((), ())), preferred_element_type=jnp.float32)


def attend_kernel(pieces, first, last, *refs):
    lengths_ref, place_ref, q_ref = refs[:3]
    count = len(pieces)
    kv_refs = refs[3 : 3 + count]
    refs = refs[3 + count :]
    if not first:
        acc_in, stat_in = refs[:2]
        refs = refs[2:]
    if last:
        out_ref = refs[0]
        refs = refs[1:]
    else:
        acc_out, stat_out = refs[:2]
        refs = refs[2:]
    v_refs = refs
    for kv_ref, v_ref in zip(kv_refs, v_refs):
        v_ref[:, :HD] = kv_ref[:, HD:]
        v_ref[:, HD:] = jnp.ones((kv_ref.shape[0], HD), jnp.bfloat16)
    lane = lax.broadcasted_iota(jnp.int32, (TILE, HD), 1)
    per = TILE // ROWS_DEV

    def row_tile(t, carry):
        index = t * TILE + lax.broadcasted_iota(jnp.int32, (TILE, 1), 0)
        planes, spots = index // (2 * ROWS_DEV), index // ROWS_DEV % 2
        rows = place_ref[0] + (planes * PLANE + spots * 2) * ROWS_DEV + index % ROWS_DEV
        start = jnp.zeros((TILE, 1), jnp.int32)
        edge = jnp.int32(0)
        for r in range(lengths_ref.shape[0]):
            edge = edge + lengths_ref[r]
            start = jnp.where(rows >= edge, edge, start)
        start = jnp.where(rows >= edge, rows, start)
        devs = pl.ds(t * per, per)
        packed = jnp.zeros((TILE, HD), jnp.float32)
        if not first:
            stat = stat_in[devs].reshape(TILE, HD)
        for h in range(HEADS):
            lanes = slice(h * HD, (h + 1) * HD)
            q = q_ref[devs, :, lanes].reshape(TILE, HD)
            if first:
                m = jnp.full((TILE, 1), -1e30, jnp.float32)
                weighted = jnp.zeros((TILE, HD), jnp.float32)
                denominator = jnp.zeros((TILE, HD), jnp.float32)
            else:
                m = stat[:, h : h + 1]
                weighted = acc_in[devs, :, lanes].reshape(TILE, HD)
                denominator = stat[:, HEADS + h : HEADS + h + 1]
            answer = 0
            for kv_ref, v_ref, spans in zip(kv_refs, v_refs, pieces):
                for low, high, masked in spans:
                    s = nt(q, kv_ref[low:high, :HD])
                    if masked:
                        answer += 1
                        column = lax.broadcasted_iota(jnp.int32, (TILE, high - low), 1)
                        keys = place_ref[answer] + column % ROWS_DEV
                        keys = keys - column // ROWS_DEV * (2 * PLANE * ROWS_DEV)
                        s = jnp.where((keys >= start) & (keys <= rows), s, -1e30)
                    raised = jnp.maximum(m, jnp.max(s, axis=1, keepdims=True))
                    shrink = jnp.exp2((m - raised) * (SCALE * LOG2E))
                    p = jnp.exp2((s - raised) * (SCALE * LOG2E)).astype(jnp.bfloat16)
                    acc = jnp.dot(p, v_ref[low:high, :], preferred_element_type=jnp.float32)
                    weighted = weighted * shrink + acc[:, :HD]
                    denominator = denominator * shrink + acc[:, HD:]
                    m = raised
            if last:
                out_ref[devs, :, lanes] = (
                    (weighted / denominator).astype(jnp.bfloat16).reshape(per, ROWS_DEV, HD)
                )
                lse = m * SCALE + jnp.log(denominator)
                high_part = lse.astype(jnp.bfloat16).astype(jnp.float32)
                middle = (lse - high_part).astype(jnp.bfloat16).astype(jnp.float32)
                low_part = lse - high_part - middle
                packed = jnp.where(lane == 3 * h, high_part, packed)
                packed = jnp.where(lane == 3 * h + 1, middle, packed)
                packed = jnp.where(lane == 3 * h + 2, low_part, packed)
            else:
                acc_out[devs, :, lanes] = weighted.reshape(per, ROWS_DEV, HD)
                packed = jnp.where(lane == h, m, packed)
                packed = jnp.where(lane == HEADS + h, denominator, packed)
        if last:
            out_ref[devs, :, HEADS * HD :] = packed.astype(jnp.bfloat16).reshape(
                per, ROWS_DEV, HD
            )
        else:
            stat_out[devs] = packed.reshape(per, ROWS_DEV, HD)
        return carry

    lax.fori_loop(0, PLANE * ROWS_DEV // TILE, row_tile, 0)


def attend(lengths, place, q, blocks, pieces, state, last):
    vmem = pl.BlockSpec(memory_space=pltpu.VMEM)
    smem = pl.BlockSpec(memory_space=pltpu.SMEM)
    keys = sum(high - low for spans in pieces for low, high, masked in spans)
    pairs = PLANE * ROWS_DEV * HEADS * keys
    if last:
        out_shape = jax.ShapeDtypeStruct((PLANE, ROWS_DEV, HEADS * HD + HD), jnp.bfloat16)
        out_specs = vmem
    else:
        out_shape = (
            jax.ShapeDtypeStruct((PLANE, ROWS_DEV, HEADS * HD), jnp.float32),
            jax.ShapeDtypeStruct((PLANE, ROWS_DEV, HD), jnp.float32),
        )
        out_specs = (vmem, vmem)
    return pl.pallas_call(
        functools.partial(attend_kernel, pieces, not state, last),
        in_specs=[smem, smem] + [vmem] * (1 + len(blocks) + len(state)),
        out_specs=out_specs,
        out_shape=out_shape,
        scratch_shapes=[pltpu.VMEM((block.shape[0], 2 * HD), jnp.bfloat16) for block in blocks],
        compiler_params=pltpu.CompilerParams(vmem_limit_bytes=40 * MIB),
        cost_estimate=pl.CostEstimate(
            flops=8 * HD * pairs, bytes_accessed=512 * keys + 2 * MIB, transcendentals=pairs
        ),
        name="attend",
    )(lengths, place, q, *blocks, *state)


def combine_kernel(parts_ref, out_ref):
    tops = []
    for j in range(PLANE):
        bits = parts_ref[j, :, HEADS * HD :].astype(jnp.float32)
        tops.append(bits + pltpu.roll(bits, HD - 1, 1) + pltpu.roll(bits, HD - 2, 1))
    top = jnp.maximum(jnp.maximum(tops[0], tops[1]), jnp.maximum(tops[2], tops[3]))
    weights = [jnp.exp(x - top) for x in tops]
    share = 1.0 / (weights[0] + weights[1] + weights[2] + weights[3])
    weights = [x * share for x in weights]
    heads = []
    for h in range(HEADS):
        lanes = slice(h * HD, (h + 1) * HD)
        heads.append(
            sum(
                weights[j][:, 3 * h : 3 * h + 1] * parts_ref[j, :, lanes].astype(jnp.float32)
                for j in range(PLANE)
            )
        )
    out_ref[...] = jnp.stack(heads, axis=1).astype(jnp.bfloat16)


def combine(parts):
    rows = 64
    return pl.pallas_call(
        combine_kernel,
        grid=(ROWS_DEV // rows,),
        in_specs=[pl.BlockSpec((PLANE, rows, HEADS * HD + HD), lambda i: (0, i, 0))],
        out_specs=pl.BlockSpec((rows, HEADS, HD), lambda i: (i, 0, 0)),
        out_shape=jax.ShapeDtypeStruct((ROWS_DEV, HEADS, HD), jnp.bfloat16),
        compiler_params=pltpu.CompilerParams(vmem_limit_bytes=62 * MIB),
        name="combine",
    )(parts)


def to_all(x, axes, count):
    return lax.all_to_all(jnp.broadcast_to(x[None], (count,) + x.shape), axes, 0, 0)


def shards(queries, prompt_kv, response_kv, logits, token_ids, lengths, rewards):
    pair = lax.axis_index("zh")
    z = lax.axis_index(Z)
    row = lax.axis_index("yl")
    core = lax.axis_index("core")
    pairs = lax.axis_size("zh")
    responses = lengths.shape[0]
    pb = prompt_kv.shape[0]
    rb = response_kv.shape[0]

    prompt = lax.all_gather(prompt_kv.reshape(pb, 2 * HD), ("zh", "core"), axis=0, tiled=True)
    q = to_all(queries.reshape(ROWS_DEV, HEADS * HD), SHARE, PLANE)

    vocab_base = (lax.axis_index("tp") * logits.shape[1]).astype(jnp.int32).reshape(1)
    stats = logit_stats(logits, token_ids, vocab_base, lax.axis_size("tp"))
    stats, q = lax.optimization_barrier((stats, q))
    stats = lax.all_to_all(stats, "tp", 0, 0)

    own = response_kv.reshape(rb, 2 * HD)
    route = [(i, (i + 1) % pairs) for i in range(pairs)]
    once = lax.ppermute(own, "zh", route)
    before = [once, lax.ppermute(once, "zh", route)]
    mine = jnp.concatenate([own] + before, axis=0)
    other = lax.ppermute(mine, "core", [(0, 1), (1, 0)])

    peaks, sums, picks = stats[:, 0], stats[:, 1], stats[:, 2]
    peak = jnp.max(peaks, axis=0)
    spread = jnp.sum(sums * jnp.exp(peaks - peak), axis=0)
    logprob = jnp.sum(picks, axis=0) - peak - jnp.log(spread)
    ends_at = jnp.cumsum(lengths)
    block = z * PLANE + row * 2
    rows = (block + core) * ROWS_DEV + jnp.arange(ROWS_DEV, dtype=jnp.int32)
    segment = jnp.sum((rows[:, None] >= ends_at[None, :]).astype(jnp.int32), axis=1)
    token_logprob = jnp.where(segment < responses, logprob, 0.0)
    members = segment[:, None] == jnp.arange(128, dtype=jnp.int32)[None, :]
    part = jnp.sum(jnp.where(members, token_logprob[:, None], 0.0), axis=0)
    part = jnp.sum(to_all(part[None], ("zl", "yl", "core"), 8)[:, 0], axis=0)

    first_row = (pair * 2 * PLANE + core) * ROWS_DEV
    place = jnp.stack(
        [first_row, (block + core) * ROWS_DEV, (block + 1 - core) * ROWS_DEV]
    ).astype(jnp.int32)
    masked = ((0, 3 * rb, True),)
    state = attend(lengths, place, q, [mine, other], [masked, masked], (), False)
    half = prompt.shape[0] // 2
    part, _ = lax.optimization_barrier((part, state[1]))
    part = jnp.sum(to_all(part[None], "zh", pairs)[:, 0], axis=0)
    spans = ((0, half, False), (half, 2 * half, False))
    partial = attend(lengths, place, q, [prompt], [spans], state, True)
    exchanged = lax.all_to_all(partial, SHARE, 0, 0)
    context = combine(exchanged)

    response_sum = part[:responses]
    length_float = lengths.astype(jnp.float32)
    adjusted = rewards - 0.5 * length_float / 2048
    advantage = adjusted - jnp.mean(adjusted)
    response_objective = -advantage * response_sum / length_float
    return (context, token_logprob, response_objective)


def solution(mesh):
    fine = Mesh(mesh.devices.reshape(8, 2, 2, 2, 8), ("zh", "zl", "yl", "core", "tp"))
    return jax.shard_map(
        shards,
        mesh=fine,
        in_specs=(
            P(CTX, "tp", None),
            P(CTX, None, "tp", None),
            P(CTX, None, "tp", None),
            P(CTX, "tp"),
            P(CTX),
            P(),
            P(),
        ),
        out_specs=(P(CTX, "tp", None), P(CTX), P()),
        check_vma=False,
    )
```
